128 devices in a mesh: oy: 8 (over x, core), ox: 16 (over y, z).
Axes of the slice: x: 4, y: 4, z: 4, core: 2. Of those that a mesh axis runs over, the one named last changes fastest.
Arguments:
- atm_flux: bfloat16 [8192, 4, 128], P(('oy', 'ox')), may hold values from -6 to 6
- remap_weights: bfloat16 [49152, 128, 128], P(('oy', 'ox')), may hold values from -0.5 to 0.5
- link_source: int32 [49152], P(('oy', 'ox')), may hold values from 0 to 63
- link_owner: int32 [49152, 1], P(('oy', 'ox')), may hold values from 0 to 127; in each aligned block of 384 rows (0 to 383, 384 to 767, ...) at most 6 rows name the same one
- link_block: int32 [49152], P(('oy', 'ox')), may hold values from 0 to 63
- ocean_mask: int32 [256, 4096], P('oy', 'ox'), may hold values 0 or 1
- level_count: int32 [256, 4096], P('oy', 'ox'), may hold values from 1 to 20
- tracers: float32 [4, 20, 256, 4096], P(None, None, 'oy', 'ox'), may hold values from -6 to 6
- diffusivity: float32 [20, 256, 4096], P(None, 'oy', 'ox'), may hold values from 0.05 to 5
- viscosity: float32 [20, 256, 4096], P(None, 'oy', 'ox'), may hold values from 0.003 to 0.025
Outputs:
- tracers_out: float32 [4, 20, 256, 4096], P(None, None, 'oy', 'ox')
- ocean_flux: float32 [4, 256, 4096], P(None, 'oy', 'ox')
The draws below stay inside these ranges and needn't reach their ends.
Inputs may be any that keep to these rules, and one draw needn't show every extreme that they name: `link_owner`: among the 384 links of one device no tile is named more than 6 times, a bound that some block reaches.
All inputs are finite; a program needn't handle non-finite values. No bound on the sum of `ocean_mask` on one device may be relied on, other than what follows from the above.
Results may differ from the reference program's by a relative error of at most 0.0003.
Values sent between devices are 32-bit elements; how exact they have to be, the bound alone decides.
No kernel may reach another device: no remote copies, remote signals or barrier semaphores. Data moves between devices by JAX's collectives and lax.ppermute only.
A program may use at most 128 MiB of HBM per device.

```python
import math
import jax
import jax.numpy as jnp
import numpy as np
from jax import lax

NTR = 4
BLK = 128
L = 20
SUBSTEPS = 2
CY = 32
CX = 256
ATM_DEV = 64
LINK_DEV = 384
NY = 256
NX = 4096
OBLK = 64
CAP = 6
LINKS = 49152
ATM_BLOCKS = 8192
N_OY = 8
N_OX = 16
DEVICES = 128


def place_ends(values, rng, low, largest):
    longest = values.shape.index(max(values.shape))
    spots = []
    for shift in (0, 1):
        where = [jax.random.randint(jax.random.fold_in(rng, axis), (), 0, length) for axis, length in enumerate(values.shape)]
        where[longest] = (where[longest] + shift) % values.shape[longest]
        spots.append(tuple(where))
    return values.at[spots[0]].set(low).at[spots[1]].set(largest)


def level_of(key, extent, cuts, smallest, largest):
    def one(position, shards_of):
        steps = jax.random.uniform(jax.random.fold_in(jax.random.fold_in(key, 6), position), (shards_of,), jnp.float32, smallest / len(cuts), largest / len(cuts))
        return jnp.repeat(jnp.exp(steps), extent[position] // shards_of).reshape((-1,) + (1,) * (len(extent) - position - 1))

    level = one(*cuts[0])
    for cut in cuts[1:]:
        level = level * one(*cut)
    return level


def shared_out(key, own, number, rows, count, top, limit, skew):
    sequence = jax.random.permutation(key, count)
    heavy_load, usual = shares(count, rows * top, limit, skew, True), shares(count, rows * top, limit, skew, False)
    places = jnp.arange(count)

    def named(sizes, turn):
        used = int((sizes > 0).sum())
        fixed = max(1, used // 4)
        passed = fixed + (places - fixed + turn * (used - fixed)) % max(1, count - fixed)
        return jnp.zeros((count,), jnp.int32).at[sequence[jnp.where(places < fixed, places, passed)]].set(jnp.asarray(sizes, jnp.int32))

    sizes = jnp.where(number % 4 == 0, named(heavy_load, number // 4), named(usual, number - number // 4 - 1))
    mixed = jax.random.permutation(jax.random.fold_in(own, 3), count)
    source_of, taker = mixed[0:count // 2 * 2:2], mixed[1:count // 2 * 2:2]
    room = jnp.minimum(sizes[source_of] - 1, limit - sizes[taker]) // 2
    room = jnp.where((source_of == sequence[0]) | (taker == sequence[0]) | (sizes[taker] == 0), 0, jnp.maximum(room, 0))
    passed = jax.random.randint(jax.random.fold_in(own, 4), (count // 2,), 0, 1 << 20) % (room + 1)
    sizes = sizes.at[source_of].add(-passed).at[taker].add(passed)
    members = jnp.searchsorted(jnp.cumsum(sizes), jnp.arange(rows * top), side="right").astype(jnp.int32)
    table = members.reshape(top, rows).T
    table = table[jax.random.permutation(jax.random.fold_in(own, 1), rows)]
    turn = jax.random.randint(jax.random.fold_in(own, 2), (rows, 1), 0, top)
    return jnp.take_along_axis(table, (jnp.arange(top)[None, :] + turn) % top, axis=1)


def shares(amount, total, reach, slope, full):
    portions = [(1 << 20) // math.isqrt(rank ** slope) + 1 for rank in range(1, amount + 1)]
    largest = reach if full else min(reach, max(-(-total // amount), total * portions[0] // sum(portions)))
    least = 1 if total - largest >= amount - 1 else 0
    counts, spare = [largest] + [least] * (amount - 1), total - largest - least * (amount - 1)
    while spare > 0:
        movable = [i for i in range(1, amount) if counts[i] < largest] or [i for i in range(1, amount) if counts[i] < reach]
        whole, budget = sum([portions[i] for i in movable]), spare
        for i in movable:
            addition = min(reach - counts[i], max(1, budget * portions[i] // whole), spare)
            counts[i] = counts[i] + addition
            spare = spare - addition
    return np.array(counts)


def noise(rng, shape, scale, most, shards=(), kind=jnp.bfloat16):
    drawn = scale * jax.random.normal(rng, shape, jnp.float32)
    if shards:
        drawn = drawn * level_of(rng, shape, shards, -0.22, 0.18)
    return jnp.clip(drawn, -most, most).astype(kind)


def setup_inputs(seed: int = 0) -> dict:
    arg_keys = jax.random.split(jax.random.key(seed), 11)
    atm_flux = noise(arg_keys[0], (ATM_BLOCKS, NTR, BLK), 1.0, 6.0, ((0, 128),))
    remap_weights = noise(arg_keys[1], (LINKS, BLK, BLK), BLK ** -0.5, 0.5, ((0, 128),))
    link_source = place_ends(jax.random.randint(arg_keys[2], (LINKS,), 0, ATM_DEV), jax.random.fold_in(arg_keys[2], 1), 0, ATM_DEV - 1).astype(jnp.int32)
    link_owner_keys = jax.random.split(jax.random.fold_in(arg_keys[3], 1), LINKS // LINK_DEV)
    link_owner_turns = jax.random.permutation(jax.random.fold_in(arg_keys[3], 3), LINKS // LINK_DEV)
    link_owner = jax.vmap(lambda own, number: shared_out(jax.random.fold_in(arg_keys[3], 2), own, number, LINK_DEV, DEVICES, 1, CAP, 2))(link_owner_keys, link_owner_turns).reshape((LINKS, 1))
    link_block = place_ends(jax.random.randint(arg_keys[4], (LINKS,), 0, OBLK), jax.random.fold_in(arg_keys[4], 1), 0, OBLK - 1).astype(jnp.int32)
    ocean_mask = place_ends((jax.random.randint(arg_keys[5], (NY, NX), 0, 4) < 3).astype(jnp.int32), jax.random.fold_in(arg_keys[5], 1), 0, 1)
    level_count = place_ends(jax.random.randint(arg_keys[6], (NY, NX), 1, L + 1), jax.random.fold_in(arg_keys[6], 1), 1, L).astype(jnp.int32)
    tracers = noise(arg_keys[7], (NTR, L, NY, NX), 1.0, 6.0, ((2, 8), (3, 16)), jnp.float32)
    diffusivity = jnp.clip(jnp.exp(math.log(5.0) - 4.6051702 * jax.random.uniform(arg_keys[8], (L, NY, NX), jnp.float32) ** level_of(arg_keys[8], (L, NY, NX), ((1, 8), (2, 16)), -0.2, 0.2)), 0.05, 5.0)
    viscosity = jnp.clip(jnp.exp(math.log(0.025) - 2.1202635 * jax.random.uniform(arg_keys[9], (L, NY, NX), jnp.float32) ** level_of(arg_keys[9], (L, NY, NX), ((1, 8), (2, 16)), -0.2, 0.2)), 0.003, 0.025)
    return {"atm_flux": atm_flux, "remap_weights": remap_weights, "link_source": link_source, "link_owner": link_owner, "link_block": link_block, "ocean_mask": ocean_mask, "level_count": level_count, "tracers": tracers, "diffusivity": diffusivity, "viscosity": viscosity}


def laplace(padded):
    return (padded[..., :-2, 1:-1] + padded[..., 2:, 1:-1] + padded[..., 1:-1, :-2]
            + padded[..., 1:-1, 2:] - 4.0 * padded[..., 1:-1, 1:-1])


def extend(field, width):
    wrapped = jnp.concatenate([field[..., -width:], field, field[..., :width]], axis=-1)
    blank = jnp.zeros(wrapped.shape[:-2] + (width, wrapped.shape[-1]), wrapped.dtype)
    return jnp.concatenate([blank, wrapped, blank], axis=-2)


def mix_columns(forced, diffusivity, levels):
    count = forced.shape[1]
    nothing = jnp.zeros(levels.shape, jnp.float32)
    couplings = [jnp.where(level + 1 < levels, diffusivity[level], nothing) for level in range(count - 1)]
    couplings = couplings + [nothing]
    sweep_ratio = nothing
    sweep_value = jnp.zeros(forced[:, 0].shape, jnp.float32)
    ratio_list = []
    value_list = []
    for level in range(count):
        upper_link = couplings[level - 1] if level > 0 else nothing
        lower_link = couplings[level]
        pivot_value = 1.0 + upper_link + lower_link - (-upper_link) * sweep_ratio
        sweep_ratio = -lower_link / pivot_value
        sweep_value = (forced[:, level] + upper_link * sweep_value) / pivot_value
        ratio_list.append(sweep_ratio)
        value_list.append(sweep_value)
    result_list = [value_list[count - 1]]
    for level in range(count - 2, -1, -1):
        result_list.append(value_list[level] - ratio_list[level] * result_list[-1])
    result_list = result_list[::-1]
    return jnp.stack(result_list, axis=1)


def reference(atm_flux, remap_weights, link_source, link_owner, link_block, ocean_mask, level_count, tracers, diffusivity, viscosity):
    devices = N_OY * N_OX
    count_links = link_source.shape[0]
    link_dev = count_links // devices
    source = (jnp.arange(count_links, dtype=jnp.int32) // link_dev) * ATM_DEV + link_source
    values = atm_flux[source].reshape(devices, link_dev, NTR, BLK)
    weights_dev = remap_weights.reshape(devices, link_dev, BLK, BLK)

    def one_device(pair):
        return jnp.einsum("kfi,kij->kfj", pair[0].astype(jnp.float32), pair[1].astype(jnp.float32),
                          precision=lax.Precision.HIGHEST)

    contrib = lax.map(one_device, (values, weights_dev)).reshape(count_links, NTR, BLK)
    owner_tile = link_owner[:, 0]
    cell_index = link_block[:, None] * BLK + jnp.arange(BLK, dtype=jnp.int32)[None, :]
    lat_index = (owner_tile // N_OX)[:, None] * CY + cell_index // CX
    lon_index = (owner_tile % N_OX)[:, None] * CX + cell_index % CX
    flat_index = (lat_index * NX + lon_index).reshape(-1)
    spread = jnp.transpose(contrib, (1, 0, 2)).reshape(NTR, -1)
    surface = jnp.zeros((NTR, NY * NX), jnp.float32).at[:, flat_index].add(spread)
    ocean_flux = surface.reshape(NTR, NY, NX) * ocean_mask.astype(jnp.float32)[None]
    levels = level_count * ocean_mask
    active = jnp.where(jnp.arange(L, dtype=jnp.int32)[:, None, None] < levels[None], 1.0, 0.0).astype(jnp.float32)
    forced = tracers.at[:, 0].add(ocean_flux)
    current = mix_columns(forced, diffusivity, levels)
    weight = viscosity * active
    for substep in range(SUBSTEPS):
        first_pass = laplace(extend(current, 1))
        second = laplace(extend(weight[None] * first_pass, 1))
        current = current - active[None] * second
    return current, ocean_flux
```

```python
import functools

import jax
import jax.numpy as jnp
from jax import lax
from jax.experimental import pallas as pl
from jax.experimental.pallas import tpu as pltpu
from jax.sharding import PartitionSpec as P

SUBSTEPS = 2
CAP = 6
H = 4
CHUNKS = 12
OWN_ID = 64
NBR_ID = 72
LIMIT = 60 * 1024 * 1024

VMEM = pl.BlockSpec(memory_space=pltpu.VMEM)
SMEM = pl.BlockSpec(memory_space=pltpu.SMEM)
ANY = pl.BlockSpec(memory_space=pl.ANY)


def params():
    return pltpu.CompilerParams(vmem_limit_bytes=LIMIT)


def remap_kernel(n_ox, source, owner, block, flux, weights, payload, held, strips, count, sem):
    links = weights.shape[0]
    per = links // CHUNKS
    copies = [
        pltpu.make_async_copy(
            weights.at[pl.ds(c * per, per)], held.at[pl.ds(c * per, per)], sem.at[c]
        )
        for c in range(CHUNKS)
    ]
    for copy in copies:
        copy.start()
    devices = payload.shape[0]

    def clear(i, carry):
        payload[i] = jnp.zeros(payload.shape[1:], jnp.float32)
        strips[i] = jnp.zeros(strips.shape[1:], jnp.float32)
        count[i] = 0
        return carry

    lax.fori_loop(0, devices, clear, 0, unroll=4)
    lane = lax.broadcasted_iota(jnp.int32, (4, 128), 1)
    group = lane >> 2

    def link(k):
        tile = owner[k]
        b = block[k]
        x = flux[source[k]].astype(jnp.bfloat16)
        value = jnp.dot(x, held[k], preferred_element_type=jnp.float32)
        slot = count[tile]
        count[tile] = slot + 1
        payload[tile, slot] = value
        odd = b & 1
        column = lax.rem(tile, n_ox)
        nbr = tile - column + lax.rem(column + jnp.where(odd == 1, 1, n_ox - 1), n_ox)
        entry = slot + jnp.where(odd == 1, 0, CAP)
        moved = pltpu.roll(value, lax.rem(4 * entry + 4 * odd, 128), 1)
        ident = (b + 1).astype(jnp.float32)
        strips[tile] = jnp.where(lane == OWN_ID + slot, ident, strips[tile])
        strips[nbr] = jnp.where(
            group == entry, moved, jnp.where(lane == NBR_ID + entry, ident, strips[nbr])
        )

    unroll = 8
    for c in range(CHUNKS):
        copies[c].wait()

        def some(i, carry, c=c):
            for j in range(unroll):
                link(c * per + i * unroll + j)
            return carry

        lax.fori_loop(0, per // unroll, some, 0)

    def finish(i, carry):
        payload[i, CAP] = strips[i]
        return carry

    lax.fori_loop(0, devices, finish, 0, unroll=8)


def remap(flux, weights, source, owner, block, devices, n_ox):
    links = weights.shape[0]
    return pl.pallas_call(
        functools.partial(remap_kernel, n_ox),
        out_shape=jax.ShapeDtypeStruct((devices, CAP + 1, 4, 128), jnp.float32),
        in_specs=[SMEM, SMEM, SMEM, VMEM, ANY],
        out_specs=VMEM,
        scratch_shapes=[
            pltpu.VMEM((links, 128, 128), jnp.bfloat16),
            pltpu.VMEM((devices, 4, 128), jnp.float32),
            pltpu.SMEM((devices,), jnp.int32),
            pltpu.SemaphoreType.DMA((CHUNKS,)),
        ],
        compiler_params=params(),
        name="remap",
    )(source, owner, block, flux, weights)


def plane_of(tracers, diffusivity, viscosity, levels, p):
    nl = diffusivity.shape[0]
    nt = tracers.shape[0]
    if p < nt * nl:
        return tracers.at[p // nl, p % nl]
    if p < (nt + 1) * nl:
        return diffusivity.at[p - nt * nl]
    if p < (nt + 2) * nl:
        return viscosity.at[p - (nt + 1) * nl]
    return levels


def pack_kernel(planes, tracers, diffusivity, viscosity, levels, west, east, top, bottom):
    rows = levels.shape[0]
    width = levels.shape[1]
    group = lax.broadcasted_iota(jnp.int32, (rows, 128), 1) >> 2
    for g in range(-(-planes // 32)):
        left = jnp.zeros((rows, 128), jnp.float32)
        right = jnp.zeros((rows, 128), jnp.float32)
        for s in range(min(32, planes - 32 * g)):
            ref = plane_of(tracers, diffusivity, viscosity, levels, 32 * g + s)
            left = jnp.where(group == s, pltpu.roll(ref[:, 0:128], 4 * s, 1), left)
            right = jnp.where(
                group == s, pltpu.roll(ref[:, width - 128 : width], (4 * s + 4) % 128, 1), right
            )
            top[32 * g + s] = ref[0:H, :]
            bottom[32 * g + s] = ref[rows - H : rows, :]
        west[g] = left
        east[g] = right


def pack(tracers, diffusivity, viscosity, levels):
    nt, nl, rows, width = tracers.shape
    planes = (nt + 2) * nl + 1
    groups = -(-planes // 32)
    edge = jax.ShapeDtypeStruct((groups, rows, 128), jnp.float32)
    line = jax.ShapeDtypeStruct((planes, H, width), jnp.float32)
    return pl.pallas_call(
        functools.partial(pack_kernel, planes),
        out_shape=(edge, edge, line, line),
        in_specs=[VMEM] * 4,
        out_specs=(VMEM,) * 4,
        compiler_params=params(),
        name="pack",
    )(tracers, diffusivity, viscosity, levels)


def mix_kernel(
    planes,
    tracers, diffusivity, viscosity, levels,
    from_west, from_east, north, south, north_corner, south_corner,
    base, response, weight, levels_ext,
    diff_ext, ratios,
):
    nt, nl, rows, width = tracers.shape
    groups = from_west.shape[0]
    lane = lax.broadcasted_iota(jnp.int32, (rows, 128), 1)
    lane8 = lax.broadcasted_iota(jnp.int32, (2 * H, 128), 1)

    def target(p):
        if p < nt * nl:
            return base.at[p % nl, p // nl]
        if p < (nt + 1) * nl:
            return diff_ext.at[p - nt * nl]
        if p < (nt + 2) * nl:
            return weight.at[p - (nt + 1) * nl]
        return levels_ext

    for p in range(planes):
        g, s = p // 32, p % 32
        out = target(p)
        ref = plane_of(tracers, diffusivity, viscosity, levels, p)
        out[0:rows, 0:width] = ref[...]
        out[rows : rows + 2 * H, 0:width] = jnp.concatenate([south[p], north[p]], axis=0)

        def side(east, west, lanes):
            return jnp.where(
                lanes < H,
                pltpu.roll(east, (128 - 4 * s) % 128, 1),
                jnp.where(lanes >= 128 - H, pltpu.roll(west, (252 - 4 * s) % 128, 1), 0.0),
            )

        out[0:rows, width : width + 128] = side(from_east[g], from_west[g], lane)
        out[rows : rows + 2 * H, width : width + 128] = side(
            jnp.concatenate([south_corner[g], north_corner[g]], axis=0),
            jnp.concatenate([south_corner[groups + g], north_corner[groups + g]], axis=0),
            lane8,
        )

    across = (width + 128) // 128

    def tile(t, carry):
        r = pl.ds(pl.multiple_of((t // across) * 8, 8), 8)
        c = pl.ds(pl.multiple_of((t % across) * 128, 128), 128)
        depth = levels_ext[r, c]
        nothing = jnp.zeros((8, 128), jnp.float32)
        ratio, upper, single = nothing, nothing, nothing
        values = [nothing] * nt
        for level in range(nl):
            if level < nl - 1:
                lower = jnp.where(level + 1 < depth, diff_ext[level, r, c], 0.0)
            else:
                lower = nothing
            inverse = 1.0 / (1.0 + upper + lower + upper * ratio)
            ratio = -lower * inverse
            ratios[level] = ratio
            for f in range(nt):
                values[f] = (base[level, f, r, c] + upper * values[f]) * inverse
                base[level, f, r, c] = values[f]
            single = inverse if level == 0 else (upper * single) * inverse
            response[level, r, c] = single
            weight[level, r, c] = jnp.where(level < depth, weight[level, r, c], 0.0)
            upper = lower
        for level in range(nl - 2, -1, -1):
            ratio = ratios[level]
            for f in range(nt):
                values[f] = base[level, f, r, c] - ratio * values[f]
                base[level, f, r, c] = values[f]
            single = response[level, r, c] - ratio * single
            response[level, r, c] = single
        return carry

    lax.fori_loop(0, (rows + 2 * H) // 8 * across, tile, 0)


def mix(tracers, diffusivity, viscosity, levels, halo):
    nt, nl, rows, width = tracers.shape
    planes = (nt + 2) * nl + 1
    tall, wide = rows + 2 * H, width + 128
    f32 = jnp.float32
    return pl.pallas_call(
        functools.partial(mix_kernel, planes),
        out_shape=(
            jax.ShapeDtypeStruct((nl, nt, tall, wide), f32),
            jax.ShapeDtypeStruct((nl, tall, wide), f32),
            jax.ShapeDtypeStruct((nl, tall, wide), f32),
            jax.ShapeDtypeStruct((tall, wide), f32),
        ),
        in_specs=[VMEM] * 10,
        out_specs=(VMEM,) * 4,
        scratch_shapes=[pltpu.VMEM((nl, tall, wide), f32), pltpu.VMEM((nl, 8, 128), f32)],
        compiler_params=params(),
        name="mix",
    )(tracers, diffusivity, viscosity, levels, *halo)


def two(x):
    high = x.astype(jnp.bfloat16)
    return high, (x - high.astype(jnp.float32)).astype(jnp.bfloat16)


def collect_kernel(arrived, mask, ocean_flux, side, to_north, to_south):
    rows, width = mask.shape
    nt = ocean_flux.shape[0]
    stride = (CAP + 1) * nt
    devices = arrived.shape[0] // stride

    def slot(s):
        return jnp.concatenate(
            [arrived[pl.ds(s * nt + f, devices, stride=stride), :] for f in range(nt)], axis=1
        )

    idents = jnp.transpose(arrived[pl.ds(CAP * nt, devices, stride=stride), :]).astype(jnp.int32) - 1
    y = lax.broadcasted_iota(jnp.int32, (rows, devices), 0)
    places = jnp.concatenate([2 * y, 2 * y + 1], axis=0)
    total = jnp.zeros((2 * rows, nt * 128), jnp.float32)
    for s in range(CAP):
        pick = (places == idents[OWN_ID + s : OWN_ID + s + 1, :]).astype(jnp.bfloat16)
        for piece in two(slot(s)):
            total = total + jnp.dot(pick, piece, preferred_element_type=jnp.float32)
    keep = mask[...].astype(jnp.float32)
    main = []
    for f in range(nt):
        cells = slice(f * 128, (f + 1) * 128)
        main.append(jnp.concatenate([total[0:rows, cells], total[rows:, cells]], axis=1) * keep)
        ocean_flux[f] = main[f]
    pick = jnp.concatenate(
        [
            (y == (idents[NBR_ID + e : NBR_ID + e + 1, :] >> 1)).astype(jnp.bfloat16)
            for e in range(2 * CAP)
        ],
        axis=0,
    )
    high, low = two(slot(CAP))
    spread = jnp.dot(pick, high, preferred_element_type=jnp.float32) + jnp.dot(
        pick, low, preferred_element_type=jnp.float32
    )
    lane = lax.broadcasted_iota(jnp.int32, (rows, 128), 1)
    for f in range(nt):
        west = jnp.zeros((rows, 128), jnp.float32)
        east = jnp.zeros((rows, 128), jnp.float32)
        for e in range(CAP):
            part = spread[e * rows : (e + 1) * rows, f * 128 : (f + 1) * 128]
            west = west + pltpu.roll(part, (124 - 4 * e) % 128, 1)
            e = e + CAP
            part = spread[e * rows : (e + 1) * rows, f * 128 : (f + 1) * 128]
            east = east + pltpu.roll(part, (128 - 4 * e) % 128, 1)
        edge = jnp.where(lane < H, east, jnp.where(lane >= 128 - H, west, 0.0))
        side[f] = edge
        whole = jnp.concatenate([main[f], edge], axis=1)
        to_north[f] = whole[0:H]
        to_south[f] = whole[rows - H : rows]


def collect(arrived, mask, nt):
    rows, width = mask.shape
    f32 = jnp.float32
    line = jax.ShapeDtypeStruct((nt, H, width + 128), f32)
    return pl.pallas_call(
        collect_kernel,
        out_shape=(
            jax.ShapeDtypeStruct((nt, rows, width), f32),
            jax.ShapeDtypeStruct((nt, rows, 128), f32),
            line,
            line,
        ),
        in_specs=[VMEM] * 2,
        out_specs=(VMEM,) * 4,
        compiler_params=params(),
        name="collect",
    )(arrived, mask)


def laplace(v):
    tall, wide = v.shape
    return (
        pltpu.roll(v, 1, 0)
        + pltpu.roll(v, tall - 1, 0)
        + pltpu.roll(v, 1, 1)
        + pltpu.roll(v, wide - 1, 1)
        - 4.0 * v
    )


def diffuse_kernel(base, response, weight, levels, main, side, north, south, out, surface):
    nt, rows, width = main.shape
    level = pl.program_id(0)

    @pl.when(level == 0)
    def _():
        wet = levels[...] > 0.0
        for f in range(nt):
            top = jnp.concatenate([main[f], side[f]], axis=1)
            whole = jnp.concatenate([top, south[f], north[f]], axis=0)
            surface[f] = jnp.where(wet, whole, 0.0)

    active = (level.astype(jnp.float32) < levels[...]).astype(jnp.float32)
    for f in range(nt):
        v = base[0, f] + response[0] * surface[f]
        for substep in range(SUBSTEPS):
            v = v - active * laplace(weight[0] * laplace(v))
        out[f, 0] = v[0:rows, 0:width]


def diffuse(base, response, weight, levels, main, side, north, south):
    nl, nt, tall, wide = base.shape
    rows, width = main.shape[1:]

    def whole(x):
        return pl.BlockSpec(x.shape, lambda i: (0,) * len(x.shape))

    layer = pl.BlockSpec((1, tall, wide), lambda i: (i, 0, 0))
    return pl.pallas_call(
        diffuse_kernel,
        grid=(nl,),
        out_shape=jax.ShapeDtypeStruct((nt, nl, rows, width), jnp.float32),
        in_specs=[
            pl.BlockSpec((1, nt, tall, wide), lambda i: (i, 0, 0, 0)),
            layer,
            layer,
            whole(levels),
            whole(main),
            whole(side),
            whole(north),
            whole(south),
        ],
        out_specs=pl.BlockSpec((nt, 1, rows, width), lambda i: (0, i, 0, 0)),
        scratch_shapes=[pltpu.VMEM((nt, tall, wide), jnp.float32)],
        compiler_params=params(),
        name="diffuse",
    )(base, response, weight, levels, main, side, north, south)


def body(
    atm_flux,
    remap_weights,
    link_source,
    link_owner,
    link_block,
    ocean_mask,
    level_count,
    tracers,
    diffusivity,
    viscosity,
):
    n_oy = lax.axis_size("oy")
    n_ox = lax.axis_size("ox")
    devices = n_oy * n_ox
    nt = tracers.shape[0]
    rows = tracers.shape[2]
    payload = remap(
        atm_flux.astype(jnp.float32),
        remap_weights,
        link_source,
        link_owner[:, 0],
        link_block,
        devices,
        n_ox,
    )
    arrived = lax.all_to_all(payload, ("oy", "ox"), split_axis=0, concat_axis=0, tiled=True)
    arrived = arrived.reshape(devices * (CAP + 1) * nt, 128)

    levels = (level_count * ocean_mask).astype(jnp.float32)
    eastward = [(i, (i + 1) % n_ox) for i in range(n_ox)]
    westward = [(j, i) for i, j in eastward]
    southward = [(i, i + 1) for i in range(n_oy - 1)]
    northward = [(j, i) for i, j in southward]
    west, east, top, bottom = pack(tracers, diffusivity, viscosity, levels)
    from_west = lax.ppermute(east, "ox", eastward)
    from_east = lax.ppermute(west, "ox", westward)
    north = lax.ppermute(bottom, "oy", southward)
    south = lax.ppermute(top, "oy", northward)
    both = jnp.concatenate([from_east, from_west], axis=0)
    north_corner = lax.ppermute(both[:, rows - H :], "oy", southward)
    south_corner = lax.ppermute(both[:, :H], "oy", northward)
    halo = (from_west, from_east, north, south, north_corner, south_corner)
    base, response, weight, levels_ext = mix(tracers, diffusivity, viscosity, levels, halo)

    ocean_flux, side, to_north, to_south = collect(arrived, ocean_mask, nt)
    flux_north = lax.ppermute(to_south, "oy", southward)
    flux_south = lax.ppermute(to_north, "oy", northward)
    mixed = diffuse(
        base, response, weight, levels_ext, ocean_flux, side, flux_north, flux_south
    )
    return mixed, ocean_flux


def solution(mesh):
    placed = (
        P(("oy", "ox"), None, None),
        P(("oy", "ox"), None, None),
        P(("oy", "ox")),
        P(("oy", "ox"), None),
        P(("oy", "ox")),
        P("oy", "ox"),
        P("oy", "ox"),
        P(None, None, "oy", "ox"),
        P(None, "oy", "ox"),
        P(None, "oy", "ox"),
    )
    return jax.shard_map(
        body,
        mesh=mesh,
        in_specs=placed,
        out_specs=(P(None, None, "oy", "ox"), P(None, "oy", "ox")),
        check_vma=False,
    )
```

```python
import functools

import jax
import jax.numpy as jnp
from jax import lax
from jax.experimental import pallas as pl
from jax.experimental.pallas import tpu as pltpu
from jax.sharding import PartitionSpec as P

SUBSTEPS = 2
CAP = 6
H = 4
CHUNKS = 12
OWN_ID = 64
NBR_ID = 72
MIB = 1024 * 1024

VMEM = pl.BlockSpec(memory_space=pltpu.VMEM)
SMEM = pl.BlockSpec(memory_space=pltpu.SMEM)
ANY = pl.BlockSpec(memory_space=pl.ANY)
F32 = jnp.float32
BF16 = jnp.bfloat16


def params(mib):
    return pltpu.CompilerParams(vmem_limit_bytes=mib * MIB)


def shaped(*shape):
    return jax.ShapeDtypeStruct(shape, F32)


def remap_kernel(
    n_ox, source, owner, block, owner_row, block_row, flux, weights,
    payload, held, flux32, table, strips, count, sem,
):
    links = weights.shape[0]
    per = links // CHUNKS
    copies = [
        pltpu.make_async_copy(
            weights.at[pl.ds(c * per, per)], held.at[pl.ds(c * per, per)], sem.at[c]
        )
        for c in range(CHUNKS)
    ]
    for copy in copies:
        copy.start()
    devices = payload.shape[0]
    flux32[...] = flux[...].astype(F32)

    owners = owner_row[...]
    blocks = block_row[...]
    tiles = lax.broadcasted_iota(jnp.int32, (devices, links), 0)
    mine = tiles == owners
    onehot = mine.astype(BF16)
    before = (
        lax.broadcasted_iota(jnp.int32, (links, links), 0)
        < lax.broadcasted_iota(jnp.int32, (links, links), 1)
    ).astype(BF16)
    ranks = jnp.dot(onehot, before, preferred_element_type=F32)
    rank = jnp.sum(jnp.where(mine, ranks, 0.0), axis=0, keepdims=True).astype(jnp.int32)
    odds = blocks & 1
    columns = lax.rem(owners, n_ox)
    nbrs = owners - columns + lax.rem(columns + jnp.where(odds == 1, 1, n_ox - 1), n_ox)
    entries = rank + jnp.where(odds == 1, 0, CAP)
    idents = (blocks + 1).astype(F32)
    spot = lax.broadcasted_iota(jnp.int32, (128, links), 0)
    across = (((1,), (1,)), ((), ()))
    table[...] = lax.dot_general(
        onehot,
        jnp.where(spot == OWN_ID + rank, idents, 0.0).astype(BF16),
        across,
        preferred_element_type=F32,
    ) + lax.dot_general(
        (tiles == nbrs).astype(BF16),
        jnp.where(spot == NBR_ID + entries, idents, 0.0).astype(BF16),
        across,
        preferred_element_type=F32,
    )

    def clear(i, carry):
        payload[i] = jnp.zeros(payload.shape[1:], F32)
        strips[i] = jnp.broadcast_to(table[pl.ds(i, 1), :], (4, 128))
        count[i] = 0
        return carry

    lax.fori_loop(0, devices, clear, 0, unroll=4)
    group = lax.broadcasted_iota(jnp.int32, (4, 128), 1) >> 2
    unroll = 16

    def links_of(start):
        waiting = []
        for j in range(unroll):
            k = start + j
            x = flux32[source[k]].astype(BF16)
            waiting.append(jnp.dot(x, held[k], preferred_element_type=F32))
        moves = []
        for j in range(unroll):
            k = start + j
            tile = owner[0, k]
            slot = count[tile]
            count[tile] = slot + 1
            payload[tile, slot] = waiting[j]
            odd = block[k] & 1
            column = lax.rem(tile, n_ox)
            nbr = tile - column + lax.rem(column + jnp.where(odd == 1, 1, n_ox - 1), n_ox)
            entry = slot + jnp.where(odd == 1, 0, CAP)
            moved = pltpu.roll(waiting[j], lax.rem(4 * entry + 4 * odd, 128), 1)
            moves.append((nbr, entry, moved))
        for nbr, entry, moved in moves:
            strips[nbr] = jnp.where(group == entry, moved, strips[nbr])

    for c in range(CHUNKS):
        copies[c].wait()

        def some(i, carry, c=c):
            links_of(c * per + i * unroll)
            return carry

        lax.fori_loop(0, per // unroll, some, 0)

    def finish(i, carry):
        payload[i, CAP] = strips[i]
        return carry

    lax.fori_loop(0, devices, finish, 0, unroll=8)


def remap(flux, weights, source, owner, block, devices, n_ox):
    links = weights.shape[0]
    owner = owner.T
    return pl.pallas_call(
        functools.partial(remap_kernel, n_ox),
        out_shape=shaped(devices, CAP + 1, 4, 128),
        in_specs=[SMEM, SMEM, SMEM, VMEM, VMEM, VMEM, ANY],
        out_specs=VMEM,
        scratch_shapes=[
            pltpu.VMEM((links, 128, 128), BF16),
            pltpu.VMEM(flux.shape, F32),
            pltpu.VMEM((devices, 128), F32),
            pltpu.VMEM((devices, 4, 128), F32),
            pltpu.SMEM((devices,), jnp.int32),
            pltpu.SemaphoreType.DMA((CHUNKS,)),
        ],
        compiler_params=params(60),
        name="remap",
    )(source, owner, block, owner, block.reshape(1, links), flux, weights)


def mix_kernel(
    tracers, diffusivity, viscosity, mask, count,
    base, response, weight, levels, west, east, top, bottom,
    ratios,
):
    nt, nl, rows, width = tracers.shape
    levels[...] = (count[...] * mask[...]).astype(F32)
    across = width // 128

    def tile(t, carry):
        r = pl.ds(pl.multiple_of((t // across) * 8, 8), 8)
        c = pl.ds(pl.multiple_of((t % across) * 128, 128), 128)
        depth = levels[r, c]
        nothing = jnp.zeros((8, 128), F32)
        ratio, upper, single = nothing, nothing, nothing
        values = [nothing] * nt
        for level in range(nl):
            if level < nl - 1:
                lower = jnp.where(level + 1 < depth, diffusivity[level, r, c], 0.0)
            else:
                lower = nothing
            inverse = 1.0 / (1.0 + upper + lower + upper * ratio)
            ratio = -lower * inverse
            ratios[level] = ratio
            for f in range(nt):
                values[f] = (tracers[f, level, r, c] + upper * values[f]) * inverse
                base[f, level, r, c] = values[f]
            single = inverse if level == 0 else (upper * single) * inverse
            response[level, r, c] = single
            weight[level, r, c] = jnp.where(level < depth, viscosity[level, r, c], 0.0)
            upper = lower
        for level in range(nl - 2, -1, -1):
            ratio = ratios[level]
            for f in range(nt):
                values[f] = base[f, level, r, c] - ratio * values[f]
                base[f, level, r, c] = values[f]
            single = response[level, r, c] - ratio * single
            response[level, r, c] = single
        return carry

    lax.fori_loop(0, rows // 8 * across, tile, 0)

    group = lax.broadcasted_iota(jnp.int32, (rows, 128), 1) >> 2
    planes = (nt + 2) * nl + 1
    for g in range(-(-planes // 32)):
        left = jnp.zeros((rows, 128), F32)
        right = jnp.zeros((rows, 128), F32)
        for s in range(min(32, planes - 32 * g)):
            p = 32 * g + s
            ref = plane_of(base, response, weight, levels, p)
            left = jnp.where(group == s, pltpu.roll(ref[:, 0:128], 4 * s, 1), left)
            right = jnp.where(
                group == s, pltpu.roll(ref[:, width - 128 : width], (4 * s + 4) % 128, 1), right
            )
            top[p] = ref[0:H, :]
            bottom[p] = ref[rows - H : rows, :]
        west[g] = left
        east[g] = right


def plane_of(base, response, weight, levels, p):
    nt, nl = base.shape[:2]
    if p < nt * nl:
        return base.at[p // nl, p % nl]
    if p < (nt + 1) * nl:
        return response.at[p - nt * nl]
    if p < (nt + 2) * nl:
        return weight.at[p - (nt + 1) * nl]
    return levels


def mix(tracers, diffusivity, viscosity, mask, count):
    nt, nl, rows, width = tracers.shape
    planes = (nt + 2) * nl + 1
    groups = -(-planes // 32)
    out = (
        shaped(nt, nl, rows, width),
        shaped(nl, rows, width),
        shaped(nl, rows, width),
        shaped(rows, width),
        shaped(groups, rows, 128),
        shaped(groups, rows, 128),
        shaped(planes + groups, H, width),
        shaped(planes + groups, H, width),
    )
    return pl.pallas_call(
        mix_kernel,
        out_shape=out,
        in_specs=[VMEM] * 5,
        out_specs=(VMEM,) * len(out),
        scratch_shapes=[pltpu.VMEM((nl, 8, 128), F32)],
        compiler_params=params(16),
        name="mix",
    )(tracers, diffusivity, viscosity, mask, count)


def middle(left, right, lane):
    return jnp.where(lane >= 64, left, right)


def spread_middle(mid, lane, nt):
    out = pltpu.roll(mid, 12, 1)
    for f in range(1, nt):
        out = jnp.where((lane >> 5) == f, pltpu.roll(mid, 32 * f + 12, 1), out)
    return out


def arrange_kernel(
    base, response, weight, levels,
    from_west, from_east, north, south,
    jobs, responses, weights, depth,
):
    nt, nl, rows, width = base.shape
    tall = rows + 2 * H
    planes = (nt + 2) * nl + 1
    lane = lax.broadcasted_iota(jnp.int32, (tall, 128), 1)

    def whole(p):
        g, s = p // 32, p % 32
        ref = plane_of(base, response, weight, levels, p)
        full = jnp.concatenate([ref[...], jnp.concatenate([south[p], north[p]], axis=0)], axis=0)
        corner = jnp.concatenate([south[planes + g], north[planes + g]], axis=0)
        west = jnp.concatenate([from_west[g], corner[:, 0:128]], axis=0)
        east = jnp.concatenate([from_east[g], corner[:, 128:256]], axis=0)
        left, right = full[:, 0:128], full[:, width - 128 : width]
        mid = middle(left, right, lane)
        left = jnp.where(lane >= 128 - H, pltpu.roll(west, (252 - 4 * s) % 128, 1), left)
        right = jnp.where(lane < H, pltpu.roll(east, (128 - 4 * s) % 128, 1), right)
        return left, right, mid

    half = nl - 16
    for level in range(nl):
        block, i = level // 8, level % 8
        packed = jnp.zeros((tall, 128), F32)
        for f in range(nt):
            left, right, mid = whole(f * nl + level)
            packed = jnp.where((lane >> 5) == f, pltpu.roll(mid, (32 * f + 12) % 128, 1), packed)
            if block < 2:
                group, place = 2 * f + block, i
            else:
                group, place = 8 + f // 2, (f % 2) * half + i
            jobs[3 + group, pl.ds(place * tall, tall), :] = left
            jobs[13 + group, pl.ds(place * tall, tall), :] = right
        jobs[block, pl.ds(i * tall, tall), :] = packed
        if block == 2:
            jobs[block, pl.ds((half + i) * tall, tall), :] = packed
        for q, out in ((nt, responses), (nt + 1, weights)):
            left, right, mid = whole(q * nl + level)
            spread = spread_middle(mid, lane, nt)
            for at in (level,) if block < 2 else (level, level + half):
                out[0, pl.ds(at * tall, tall), :] = spread
                out[1, pl.ds(at * tall, tall), :] = left
                out[2, pl.ds(at * tall, tall), :] = right
    left, right, mid = whole((nt + 2) * nl)
    depth[0] = spread_middle(mid, lane, nt)
    depth[1] = left
    depth[2] = right


def arrange(base, response, weight, levels, halo):
    nt, nl, rows, width = base.shape
    tall = rows + 2 * H
    out = (
        shaped(23, 8 * tall, 128),
        shaped(3, 24 * tall, 128),
        shaped(3, 24 * tall, 128),
        shaped(3, tall, 128),
    )
    return pl.pallas_call(
        arrange_kernel,
        out_shape=out,
        in_specs=[VMEM] * (4 + len(halo)),
        out_specs=(VMEM,) * 4,
        compiler_params=params(20),
        name="arrange",
    )(base, response, weight, levels, *halo)


def two(x):
    high = x.astype(jnp.bfloat16)
    return high, (x - high.astype(jnp.float32)).astype(jnp.bfloat16)


def collect_kernel(arrived, mask, ocean_flux, side, to_north, to_south):
    rows, width = mask.shape
    nt = ocean_flux.shape[0]
    stride = (CAP + 1) * nt
    devices = arrived.shape[0] // stride

    def slot(s):
        return jnp.concatenate(
            [arrived[pl.ds(s * nt + f, devices, stride=stride), :] for f in range(nt)], axis=1
        )

    idents = jnp.transpose(arrived[pl.ds(CAP * nt, devices, stride=stride), :]).astype(jnp.int32) - 1
    y = lax.broadcasted_iota(jnp.int32, (rows, devices), 0)
    places = jnp.concatenate([2 * y, 2 * y + 1], axis=0)
    total = jnp.zeros((2 * rows, nt * 128), jnp.float32)
    for s in range(CAP):
        pick = (places == idents[OWN_ID + s : OWN_ID + s + 1, :]).astype(jnp.bfloat16)
        for piece in two(slot(s)):
            total = total + jnp.dot(pick, piece, preferred_element_type=jnp.float32)
    keep = mask[...].astype(jnp.float32)
    main = []
    for f in range(nt):
        cells = slice(f * 128, (f + 1) * 128)
        main.append(jnp.concatenate([total[0:rows, cells], total[rows:, cells]], axis=1) * keep)
        ocean_flux[f] = main[f]
    pick = jnp.concatenate(
        [
            (y == (idents[NBR_ID + e : NBR_ID + e + 1, :] >> 1)).astype(jnp.bfloat16)
            for e in range(2 * CAP)
        ],
        axis=0,
    )
    high, low = two(slot(CAP))
    spread = jnp.dot(pick, high, preferred_element_type=jnp.float32) + jnp.dot(
        pick, low, preferred_element_type=jnp.float32
    )
    lane = lax.broadcasted_iota(jnp.int32, (rows, 128), 1)
    for f in range(nt):
        west = jnp.zeros((rows, 128), jnp.float32)
        east = jnp.zeros((rows, 128), jnp.float32)
        for e in range(CAP):
            part = spread[e * rows : (e + 1) * rows, f * 128 : (f + 1) * 128]
            west = west + pltpu.roll(part, (124 - 4 * e) % 128, 1)
            e = e + CAP
            part = spread[e * rows : (e + 1) * rows, f * 128 : (f + 1) * 128]
            east = east + pltpu.roll(part, (128 - 4 * e) % 128, 1)
        edge = jnp.where(lane < H, east, jnp.where(lane >= 128 - H, west, 0.0))
        side[f] = edge
        whole = jnp.concatenate([main[f], edge], axis=1)
        to_north[f] = whole[0:H]
        to_south[f] = whole[rows - H : rows]


def collect(arrived, mask, nt):
    rows, width = mask.shape
    f32 = jnp.float32
    line = jax.ShapeDtypeStruct((nt, H, width + 128), f32)
    return pl.pallas_call(
        collect_kernel,
        out_shape=(
            jax.ShapeDtypeStruct((nt, rows, width), f32),
            jax.ShapeDtypeStruct((nt, rows, 128), f32),
            line,
            line,
        ),
        in_specs=[VMEM] * 2,
        out_specs=(VMEM,) * 4,
        compiler_params=params(12),
        name="collect",
    )(arrived, mask)


def diffuse_kernel(
    jobs, responses, weights, depth, main, side, north, south,
    out, surface, start, done, merged, sem,
):
    nt, rows, width = main.shape
    tall = rows + 2 * H
    lane = lax.broadcasted_iota(jnp.int32, (tall, 128), 1)

    packed = jnp.zeros((tall, 128), F32)
    for f in range(nt):
        beyond = jnp.concatenate([south[f], north[f]], axis=0)
        left = jnp.concatenate([main[f, :, 0:128], beyond[:, 0:128]], axis=0)
        right = jnp.concatenate([main[f, :, 128:256], beyond[:, 128:256]], axis=0)
        edges = jnp.concatenate([side[f], beyond[:, 256:384]], axis=0)
        mid = middle(left, right, lane)
        packed = jnp.where((lane >> 5) == f, pltpu.roll(mid, (32 * f + 12) % 128, 1), packed)
        left = jnp.where(lane >= 128 - H, edges, left)
        right = jnp.where(lane < H, edges, right)
        surface[1, f] = jnp.where(depth[1] > 0.0, left, 0.0)
        surface[2, f] = jnp.where(depth[2] > 0.0, right, 0.0)
    surface[0, 0] = jnp.where(depth[0] > 0.0, packed, 0.0)

    sub = lax.broadcasted_iota(jnp.int32, (8, 128), 0)

    def row(y):
        return y if y >= 0 else y + tall

    def run(job, part, first, f0, f4):
        for i in range(8):
            at = pl.ds(i * tall, tall)
            beside = pl.ds(pl.multiple_of((first + i) * tall, 8), tall)
            start[at, :] = jobs[job, at, :] + responses[part, beside, :] * surface[
                part, f0 if i < 4 else f4
            ]
        level = (jnp.where(first == 16, sub & 3, sub) + first).astype(F32)

        def laplace(v, y):
            c = v[y]
            return (
                (v[y - 1] + v[y + 1]) + (pltpu.roll(c, 1, 1) + pltpu.roll(c, 127, 1))
            ) - 4.0 * c

        v, w, scaled, active = {}, {}, {}, {}
        for y in range(-H, rows + H):
            v[y] = start[pl.ds(row(y), 8, stride=tall), :]
            w[y] = weights[part, pl.ds(first * tall + row(y), 8, stride=tall), :]
            active[y] = level < depth[part, pl.ds(row(y), 1), :]
        now = v
        for substep in range(SUBSTEPS):
            out_of = 2 * substep + 1
            for y in range(-H + out_of, rows + H - out_of):
                scaled[substep, y] = w[y] * laplace(now, y)
            these = {y: scaled[substep, y] for y in range(-H + out_of, rows + H - out_of)}
            out_of += 1
            now = {
                y: now[y] - jnp.where(active[y], laplace(these, y), 0.0)
                for y in range(-H + out_of, rows + H - out_of)
            }
        for y in range(rows):
            done[job, pl.ds(y, 8, stride=rows), :] = now[y]

    def strips(m, carry):
        run(m, 0, 8 * m, 0, 0)
        return carry

    lax.fori_loop(0, 3, strips, 0)
    wide = lax.broadcasted_iota(jnp.int32, (rows, 128), 1)

    def send(group):
        if group < 8:
            return [(group // 2, 8 * (group % 2), 0, 8)]
        return [(2 * (group - 8), 16, 0, 4), (2 * (group - 8) + 1, 16, 4, 4)]

    def both(group, carry):
        last = group >= 8
        f0 = jnp.where(last, 2 * (group - 8), group // 2)
        f4 = jnp.where(last, f0 + 1, f0)
        first = jnp.where(last, 16, 8 * (group % 2))
        run(3 + group, 1, first, f0, f4)
        run(13 + group, 2, first, f0, f4)
        for i in range(8):
            f = f0 if i < 4 else f4
            at = pl.ds(i * rows, rows)
            strip = done[first // 8, at, :]
            turn = pltpu.roll(strip, lax.rem(244 - 32 * f, 128), 1)
            merged[group, i, :, 0:128] = jnp.where(wide < 120, done[3 + group, at, :], turn)
            turn = pltpu.roll(strip, lax.rem(244 - 32 * f, 128), 1)
            merged[group, i, :, 128:256] = jnp.where(wide >= 8, done[13 + group, at, :], turn)
        return carry

    def copies(group):
        return [
            pltpu.make_async_copy(
                merged.at[group, pl.ds(i, n)], out.at[f, pl.ds(level, n)], sem.at[group, k]
            )
            for k, (f, level, i, n) in enumerate(send(group))
        ]

    for group in range(10):
        both(jnp.int32(group), 0)
        for copy in copies(group):
            copy.start()
    for group in range(10):
        for copy in copies(group):
            copy.wait()


def diffuse(jobs, responses, weights, depth, main, side, north, south, nl):
    nt, rows, width = main.shape
    tall = rows + 2 * H
    return pl.pallas_call(
        diffuse_kernel,
        out_shape=shaped(nt, nl, rows, width),
        in_specs=[VMEM] * 8,
        out_specs=ANY,
        scratch_shapes=[
            pltpu.VMEM((3, nt, tall, 128), F32),
            pltpu.VMEM((8 * tall, 128), F32),
            pltpu.VMEM((23, 8 * rows, 128), F32),
            pltpu.VMEM((10, 8, rows, width), F32),
            pltpu.SemaphoreType.DMA((10, 2)),
        ],
        compiler_params=params(24),
        name="diffuse",
    )(jobs, responses, weights, depth, main, side, north, south)


def body(
    atm_flux,
    remap_weights,
    link_source,
    link_owner,
    link_block,
    ocean_mask,
    level_count,
    tracers,
    diffusivity,
    viscosity,
):
    n_oy = lax.axis_size("oy")
    n_ox = lax.axis_size("ox")
    devices = n_oy * n_ox
    nt, nl, rows, width = tracers.shape
    payload = remap(
        atm_flux, remap_weights, link_source, link_owner, link_block, devices, n_ox
    )
    arrived = lax.all_to_all(payload, ("oy", "ox"), split_axis=0, concat_axis=0, tiled=True)
    arrived = arrived.reshape(devices * (CAP + 1) * nt, 128)

    def moved(x, dy, dx):
        pairs = []
        for i in range(n_oy):
            for j in range(n_ox):
                if 0 <= i + dy < n_oy:
                    pairs.append((i * n_ox + j, (i + dy) * n_ox + (j + dx) % n_ox))
        return lax.ppermute(x, ("oy", "ox"), pairs)

    base, response, weight, levels, west, east, top, bottom = mix(
        tracers, diffusivity, viscosity, ocean_mask, level_count
    )
    from_west = moved(east, 0, 1)
    from_east = moved(west, 0, -1)

    def with_corners(line, first):
        corners = jnp.concatenate(
            [from_west[:, first : first + H], from_east[:, first : first + H]], axis=2
        )
        return lax.dynamic_update_slice(line, corners, (line.shape[0] - corners.shape[0], 0, 0))

    north = moved(with_corners(bottom, rows - H), 1, 0)
    south = moved(with_corners(top, 0), -1, 0)
    halo = (from_west, from_east, north, south)
    tiles = arrange(base, response, weight, levels, halo)

    ocean_flux, side, to_north, to_south = collect(arrived, ocean_mask, nt)
    flux_north = moved(to_south, 1, 0)
    flux_south = moved(to_north, -1, 0)
    mixed = diffuse(*tiles, ocean_flux, side, flux_north, flux_south, nl)
    return mixed, ocean_flux


def solution(mesh):
    placed = (
        P(("oy", "ox"), None, None),
        P(("oy", "ox"), None, None),
        P(("oy", "ox")),
        P(("oy", "ox"), None),
        P(("oy", "ox")),
        P("oy", "ox"),
        P("oy", "ox"),
        P(None, None, "oy", "ox"),
        P(None, "oy", "ox"),
        P(None, "oy", "ox"),
    )
    return jax.shard_map(
        body,
        mesh=mesh,
        in_specs=placed,
        out_specs=(P(None, None, "oy", "ox"), P(None, "oy", "ox")),
        check_vma=False,
    )
```

```python
import functools

import jax
import jax.numpy as jnp
from jax import lax
from jax.experimental import pallas as pl
from jax.experimental.pallas import tpu as pltpu
from jax.sharding import PartitionSpec as P

SUBSTEPS = 2
CAP = 6
H = 4
CHUNKS = 12
OWN_ID = 64
NBR_ID = 72
MIB = 1024 * 1024
PITCH = 40
MIX_MIB, ARRANGE_MIB, DIFFUSE_MIB = 60, 16, 24

VMEM = pl.BlockSpec(memory_space=pltpu.VMEM)
SMEM = pl.BlockSpec(memory_space=pltpu.SMEM)
ANY = pl.BlockSpec(memory_space=pl.ANY)
HBM = pl.BlockSpec(memory_space=pltpu.HBM)
F32 = jnp.float32
BF16 = jnp.bfloat16


def params(mib):
    return pltpu.CompilerParams(vmem_limit_bytes=mib * MIB)


def shaped(*shape):
    return jax.ShapeDtypeStruct(shape, F32)


def remap_kernel(
    n_ox, source, owner_row, block_row, flux, weights,
    payload, held, flux32, table, strips, codes, places, sem, sent,
):
    links = weights.shape[0]
    per = links // CHUNKS
    copies = [
        pltpu.make_async_copy(
            weights.at[pl.ds(c * per, per)], held.at[pl.ds(c * per, per)], sem.at[c]
        )
        for c in range(CHUNKS)
    ]
    for copy in copies:
        copy.start()
    devices = payload.shape[0]

    owners = owner_row[...]
    blocks = block_row[...].reshape(1, links)
    tiles = lax.broadcasted_iota(jnp.int32, (devices, links), 0)
    mine = tiles == owners
    onehot = mine.astype(BF16)
    before = (
        lax.broadcasted_iota(jnp.int32, (links, links), 0)
        < lax.broadcasted_iota(jnp.int32, (links, links), 1)
    ).astype(BF16)
    ranks = jnp.dot(onehot, before, preferred_element_type=F32)
    rank = jnp.sum(jnp.where(mine, ranks, 0.0), axis=0, keepdims=True).astype(jnp.int32)
    odds = blocks & 1
    columns = lax.rem(owners, n_ox)
    nbrs = owners - columns + lax.rem(columns + jnp.where(odds == 1, 1, n_ox - 1), n_ox)
    entries = rank + jnp.where(odds == 1, 0, CAP)
    codes[0:1, :] = owners
    codes[1:2, :] = rank
    codes[2:3, :] = nbrs
    codes[3:4, :] = entries
    codes[4:5, :] = (4 * entries + 4 * odds) & 127
    send = pltpu.make_async_copy(codes, places, sent)
    send.start()
    flux32[...] = flux[...].astype(F32)

    idents = (blocks + 1).astype(F32)
    spot = lax.broadcasted_iota(jnp.int32, (128, links), 0)
    across = (((1,), (1,)), ((), ()))
    table[...] = lax.dot_general(
        onehot,
        jnp.where(spot == OWN_ID + rank, idents, 0.0).astype(BF16),
        across,
        preferred_element_type=F32,
    ) + lax.dot_general(
        (tiles == nbrs).astype(BF16),
        jnp.where(spot == NBR_ID + entries, idents, 0.0).astype(BF16),
        across,
        preferred_element_type=F32,
    )

    def clear(i, carry):
        payload[i] = jnp.zeros(payload.shape[1:], F32)
        strips[i] = jnp.broadcast_to(table[pl.ds(i, 1), :], (4, 128))
        return carry

    lax.fori_loop(0, devices, clear, 0, unroll=4)
    send.wait()
    group = lax.broadcasted_iota(jnp.int32, (4, 128), 1) >> 2

    for c in range(CHUNKS):
        copies[c].wait()

        def chunk(_, carry, c=c):
            values, moves = [], []
            for k in range(c * per, (c + 1) * per, 2):
                two_x = jnp.concatenate([flux32[source[k]], flux32[source[k + 1]]], axis=0)
                two_w = jnp.concatenate([held[k], held[k + 1]], axis=1)
                product = jnp.dot(two_x.astype(BF16), two_w, preferred_element_type=F32)
                values += [(k, product[0:4, 0:128]), (k + 1, product[4:8, 128:256])]
            for k, value in values:
                payload[places[0, k], places[1, k]] = value
                moves.append((k, pltpu.roll(value, places[4, k], 1)))
            for k, moved in moves:
                nbr = places[2, k]
                strips[nbr] = jnp.where(group == places[3, k], moved, strips[nbr])
            return carry

        chunk(0, 0)

    def finish(i, carry):
        payload[i, CAP] = strips[i]
        return carry

    lax.fori_loop(0, devices, finish, 0, unroll=8)


def remap(flux, weights, source, owner, block, devices, n_ox):
    links = weights.shape[0]
    return pl.pallas_call(
        functools.partial(remap_kernel, n_ox),
        out_shape=shaped(devices, CAP + 1, 4, 128),
        in_specs=[SMEM, VMEM, VMEM, VMEM, ANY],
        out_specs=VMEM,
        scratch_shapes=[
            pltpu.VMEM((links, 128, 128), BF16),
            pltpu.VMEM(flux.shape, F32),
            pltpu.VMEM((devices, 128), F32),
            pltpu.VMEM((devices, 4, 128), F32),
            pltpu.VMEM((8, links), jnp.int32),
            pltpu.SMEM((8, links), jnp.int32),
            pltpu.SemaphoreType.DMA((CHUNKS,)),
            pltpu.SemaphoreType.DMA,
        ],
        compiler_params=params(60),
        name="remap",
    )(source, owner.T, block, flux, weights)


def job_place(f, level, nl):
    if level < 16:
        return 2 * f + level // 8, level % 8
    return 8 + f // 2, (f % 2) * (nl - 16) + level - 16


def level_places(level, nl):
    return (level,) if level < 16 else (level, level + nl - 16)


def middle(left, right, lane):
    return jnp.where(lane >= 64, left, right)


def spread_middle(mid, lane, nt):
    out = pltpu.roll(mid, 12, 1)
    for f in range(1, nt):
        out = jnp.where((lane >> 5) == f, pltpu.roll(mid, 32 * f + 12, 1), out)
    return out


def pack_middle(mids, lane):
    out = pltpu.roll(mids[0], 12, 1)
    for f in range(1, len(mids)):
        out = jnp.where((lane >> 5) == f, pltpu.roll(mids[f], 32 * f + 12, 1), out)
    return out


def mix_kernel(
    tracers, diffusivity, viscosity, mask, count,
    mids, sides, responses, weights, depth, west, east, top, bottom,
    ratios,
):
    nt, nl, rows, width = tracers.shape
    levels = (count[...] * mask[...]).astype(F32)
    lane = lax.broadcasted_iota(jnp.int32, (rows, 128), 1)
    depth[1] = levels[:, 0:128]
    depth[2] = levels[:, 128:256]
    depth[0] = spread_middle(middle(levels[:, 0:128], levels[:, 128:256], lane), lane, nt)
    across = width // 128

    def tile(t, carry):
        first = pl.multiple_of((t // across) * 8, 8)
        half = t % across
        r = pl.ds(first, 8)
        c = pl.ds(pl.multiple_of(half * 128, 128), 128)

        def plane(f, level):
            group, place = job_place(f, level, nl)
            return 10 * half + group, pl.ds(first + place * rows, 8)

        bottomless = depth[1 + half, r, :]
        nothing = jnp.zeros((8, 128), F32)
        ratio, upper, single = nothing, nothing, nothing
        values = [nothing] * nt
        for level in range(nl):
            if level < nl - 1:
                lower = jnp.where(level + 1 < bottomless, diffusivity[level, r, c], 0.0)
            else:
                lower = nothing
            inverse = 1.0 / (1.0 + upper + lower + upper * ratio)
            ratio = -lower * inverse
            ratios[level] = ratio
            for f in range(nt):
                values[f] = (tracers[f, level, r, c] + upper * values[f]) * inverse
                at = plane(f, level)
                sides[at[0], at[1], :] = values[f]
            single = inverse if level == 0 else (upper * single) * inverse
            weight = jnp.where(level < bottomless, viscosity[level, r, c], 0.0)
            for place in level_places(level, nl):
                responses[1 + half, pl.ds(first + place * rows, 8), :] = single
                weights[1 + half, pl.ds(first + place * rows, 8), :] = weight
            upper = lower
        for level in range(nl - 2, -1, -1):
            ratio = ratios[level]
            for f in range(nt):
                at = plane(f, level)
                values[f] = sides[at[0], at[1], :] - ratio * values[f]
                sides[at[0], at[1], :] = values[f]
            single = responses[1 + half, pl.ds(first + level * rows, 8), :] - ratio * single
            for place in level_places(level, nl):
                responses[1 + half, pl.ds(first + place * rows, 8), :] = single
        return carry

    lax.fori_loop(0, rows // 8 * across, tile, 0)

    def halves(p):
        if p < nt * nl:
            group, place = job_place(p // nl, p % nl, nl)
            at = pl.ds(place * rows, rows)
            return sides[group, at, :], sides[10 + group, at, :]
        if p < (nt + 2) * nl:
            ref = (responses, weights)[p // nl - nt]
            at = pl.ds(p % nl * rows, rows)
            return ref[1, at, :], ref[2, at, :]
        return depth[1], depth[2]

    part = lane >> 2
    planes = (nt + 2) * nl + 1
    for g in range(-(-planes // 32)):
        to_west = jnp.zeros((rows, 128), F32)
        to_east = jnp.zeros((rows, 128), F32)
        for s in range(min(32, planes - 32 * g)):
            p = 32 * g + s
            left, right = halves(p)
            to_west = jnp.where(part == s, pltpu.roll(left, 4 * s, 1), to_west)
            to_east = jnp.where(part == s, pltpu.roll(right, (4 * s + 4) % 128, 1), to_east)
            top[p, :, 0:128] = left[0:H]
            top[p, :, 128:256] = right[0:H]
            bottom[p, :, 0:128] = left[rows - H : rows]
            bottom[p, :, 128:256] = right[rows - H : rows]
        west[g] = to_west
        east[g] = to_east
    for level in range(nl):
        packed = pack_middle(
            [middle(*halves(f * nl + level), lane) for f in range(nt)], lane
        )
        for place in level_places(level, nl):
            mids[level // 8, pl.ds((place - level // 8 * 8) * rows, rows), :] = packed
        for q, ref in ((nt, responses), (nt + 1, weights)):
            spread = spread_middle(middle(*halves(q * nl + level), lane), lane, nt)
            for place in level_places(level, nl):
                ref[0, pl.ds(place * rows, rows), :] = spread


def mix(tracers, diffusivity, viscosity, mask, count):
    nt, nl, rows, width = tracers.shape
    planes = (nt + 2) * nl + 1
    groups = -(-planes // 32)
    out = (
        shaped(3, 8 * rows, 128),
        shaped(20, 8 * rows, 128),
        shaped(3, 24 * rows, 128),
        shaped(3, 24 * rows, 128),
        shaped(3, rows, 128),
        shaped(groups, rows, 128),
        shaped(groups, rows, 128),
        shaped(planes, H, width),
        shaped(planes, H, width),
    )
    return pl.pallas_call(
        mix_kernel,
        out_shape=out,
        in_specs=[VMEM] * 5,
        out_specs=(VMEM,) * len(out),
        scratch_shapes=[pltpu.VMEM((nl, 8, 128), F32)],
        compiler_params=params(MIX_MIB),
        name="mix",
    )(tracers, diffusivity, viscosity, mask, count)


def arrange_kernel(
    nt, nl,
    mids_in, sides_in, responses_in, weights_in, depth_in,
    west_in, east_in, north_in, south_in,
    mids, sides, responses, weights, depth,
    halo_jobs, halo_responses, halo_weights, halo_depth,
    from_west, from_east, north, south, sem,
):
    pairs = (
        (west_in, from_west),
        (east_in, from_east),
        (north_in, north),
        (south_in, south),
        (responses_in, responses),
        (weights_in, weights),
        (depth_in, depth),
        (sides_in, sides),
        (mids_in, mids),
    )
    copies = [pltpu.make_async_copy(a, b, sem.at[k]) for k, (a, b) in enumerate(pairs)]
    for copy in copies:
        copy.start()
    rows = depth.shape[1]
    lane = lax.broadcasted_iota(jnp.int32, (rows, 128), 1)
    lane8 = lax.broadcasted_iota(jnp.int32, (2 * H, 128), 1)

    def patch(p, ref, left, right, at):
        g, s = p // 32, p % 32
        ref[left, at, :] = jnp.where(
            lane >= 128 - H, pltpu.roll(from_west[g], (252 - 4 * s) % 128, 1), ref[left, at, :]
        )
        ref[right, at, :] = jnp.where(
            lane < H, pltpu.roll(from_east[g], (128 - 4 * s) % 128, 1), ref[right, at, :]
        )

    def beyond(p):
        both = jnp.concatenate([south[p], north[p]], axis=0)
        left, right = both[:, 0:128], both[:, 128:256]
        return left, right, middle(left, right, lane8)

    for copy in copies[:4]:
        copy.wait()
    for level in range(nl):
        packed = []
        for f in range(nt):
            group, place = job_place(f, level, nl)
            at = pl.ds(place * 8, 8)
            near, far, mid = beyond(f * nl + level)
            halo_jobs[3 + group, at, :] = near
            halo_jobs[13 + group, at, :] = far
            packed.append(mid)
        packed = pack_middle(packed, lane8)
        for place in level_places(level, nl):
            halo_jobs[level // 8, pl.ds((place - level // 8 * 8) * 8, 8), :] = packed
        for q, halo in ((nt, halo_responses), (nt + 1, halo_weights)):
            near, far, mid = beyond(q * nl + level)
            mid = spread_middle(mid, lane8, nt)
            for place in level_places(level, nl):
                at = pl.ds(place * 8, 8)
                halo[0, at, :] = mid
                halo[1, at, :] = near
                halo[2, at, :] = far
    near, far, mid = beyond((nt + 2) * nl)
    halo_depth[0] = spread_middle(mid, lane8, nt)
    halo_depth[1] = near
    halo_depth[2] = far
    for copy in copies[4:7]:
        copy.wait()
    for level in range(nl):
        for q, ref in ((nt, responses), (nt + 1, weights)):
            for place in level_places(level, nl):
                patch(q * nl + level, ref, 1, 2, pl.ds(place * rows, rows))
    patch((nt + 2) * nl, depth, 1, 2, slice(None))
    copies[7].wait()
    for level in range(nl):
        for f in range(nt):
            group, place = job_place(f, level, nl)
            patch(f * nl + level, sides, group, 10 + group, pl.ds(place * rows, rows))
    copies[8].wait()


def arrange(nt, nl, mixed, halo):
    operands = (*mixed, *halo)
    out = tuple(shaped(*x.shape) for x in mixed) + (
        shaped(23, 64, 128),
        shaped(3, 24 * 8, 128),
        shaped(3, 24 * 8, 128),
        shaped(3, 8, 128),
    )
    return pl.pallas_call(
        functools.partial(arrange_kernel, nt, nl),
        out_shape=out,
        in_specs=[HBM] * len(operands),
        out_specs=(VMEM,) * len(out),
        scratch_shapes=[pltpu.VMEM(x.shape, F32) for x in halo]
        + [pltpu.SemaphoreType.DMA((len(operands),))],
        compiler_params=params(ARRANGE_MIB),
        name="arrange",
    )(*operands)


def two(x):
    high = x.astype(jnp.bfloat16)
    return high, (x - high.astype(jnp.float32)).astype(jnp.bfloat16)


def collect_kernel(
    arrived, mask, corners, ocean_flux, side, to_north, to_south,
):
    rows, width = mask.shape
    nt = ocean_flux.shape[0]
    stride = (CAP + 1) * nt
    devices = arrived.shape[0] // stride

    def slot(s):
        return jnp.concatenate(
            [arrived[pl.ds(s * nt + f, devices, stride=stride), :] for f in range(nt)], axis=1
        )

    idents = jnp.transpose(arrived[pl.ds(CAP * nt, devices, stride=stride), :]).astype(jnp.int32) - 1
    y = lax.broadcasted_iota(jnp.int32, (rows, devices), 0)
    places = jnp.concatenate([2 * y, 2 * y + 1], axis=0)
    total = jnp.zeros((2 * rows, nt * 128), jnp.float32)
    for s in range(CAP):
        pick = (places == idents[OWN_ID + s : OWN_ID + s + 1, :]).astype(jnp.bfloat16)
        for piece in two(slot(s)):
            total = total + jnp.dot(pick, piece, preferred_element_type=jnp.float32)
    keep = mask[...].astype(jnp.float32)
    main = []
    for f in range(nt):
        cells = slice(f * 128, (f + 1) * 128)
        main.append(jnp.concatenate([total[0:rows, cells], total[rows:, cells]], axis=1) * keep)
        ocean_flux[f] = main[f]
    pick = jnp.concatenate(
        [
            (y == (idents[NBR_ID + e : NBR_ID + e + 1, :] >> 1)).astype(jnp.bfloat16)
            for e in range(2 * CAP)
        ],
        axis=0,
    )
    high, low = two(slot(CAP))
    spread = jnp.dot(pick, high, preferred_element_type=jnp.float32) + jnp.dot(
        pick, low, preferred_element_type=jnp.float32
    )
    lane = lax.broadcasted_iota(jnp.int32, (rows, 128), 1)
    for f in range(nt):
        west = jnp.zeros((rows, 128), jnp.float32)
        east = jnp.zeros((rows, 128), jnp.float32)
        for e in range(CAP):
            part = spread[e * rows : (e + 1) * rows, f * 128 : (f + 1) * 128]
            west = west + pltpu.roll(part, (124 - 4 * e) % 128, 1)
            e = e + CAP
            part = spread[e * rows : (e + 1) * rows, f * 128 : (f + 1) * 128]
            east = east + pltpu.roll(part, (128 - 4 * e) % 128, 1)
        edge = jnp.where(lane < H, east, jnp.where(lane >= 128 - H, west, 0.0))
        side[f] = edge
        for t, lanes in enumerate((main[f][:, 0:128], main[f][:, 128:256], edge)):
            to_north[3 * f + t] = lanes[0:H]
            to_south[3 * f + t] = lanes[rows - H : rows]
    groups = corners.shape[0]
    for g in range(groups):
        to_north[3 * nt + g] = corners[g, 0:H]
        to_south[3 * nt + g] = corners[g, H : 2 * H]


def collect(arrived, mask, corners, nt):
    rows, width = mask.shape
    f32 = jnp.float32
    line = shaped(3 * nt + corners.shape[0], H, 128)
    return pl.pallas_call(
        collect_kernel,
        out_shape=(
            jax.ShapeDtypeStruct((nt, rows, width), f32),
            jax.ShapeDtypeStruct((nt, rows, 128), f32),
            line,
            line,
        ),
        in_specs=[VMEM] * 3,
        out_specs=(VMEM,) * 4,
        compiler_params=params(12),
        name="collect",
    )(arrived, mask, corners)


def diffuse_kernel(
    nl,
    mids, sides, responses, weights, depth,
    halo_jobs, halo_responses, halo_weights, halo_depth, main, side, north, south,
    out, surface, surface_halo, start, start_halo, far_weights, far_depth, corners,
    done, merged, sem,
):
    nt, rows, width = main.shape
    lane = lax.broadcasted_iota(jnp.int32, (rows, 128), 1)
    lane8 = lax.broadcasted_iota(jnp.int32, (2 * H, 128), 1)
    planes = (nt + 2) * nl + 1
    groups = -(-planes // 32)
    for g in range(2 * groups):
        corners[g] = jnp.concatenate([south[3 * nt + g], north[3 * nt + g]], axis=0)

    def patched(p, left, right):
        g, s = p // 32, p % 32
        return (
            jnp.where(lane8 >= 128 - H, pltpu.roll(corners[g], (252 - 4 * s) % 128, 1), left),
            jnp.where(lane8 < H, pltpu.roll(corners[groups + g], (128 - 4 * s) % 128, 1), right),
        )

    far_depth[0] = halo_depth[0]
    far_depth[1], far_depth[2] = patched(planes - 1, halo_depth[1], halo_depth[2])

    packed, packed8 = [], []
    for f in range(nt):
        left, right = main[f, :, 0:128], main[f, :, 128:256]
        packed.append(middle(left, right, lane))
        left = jnp.where(lane >= 128 - H, side[f], left)
        right = jnp.where(lane < H, side[f], right)
        surface[1, f] = jnp.where(depth[1] > 0.0, left, 0.0)
        surface[2, f] = jnp.where(depth[2] > 0.0, right, 0.0)
        left, right, edge = [
            jnp.concatenate([south[3 * f + t], north[3 * f + t]], axis=0) for t in range(3)
        ]
        packed8.append(middle(left, right, lane8))
        left = jnp.where(lane8 >= 128 - H, edge, left)
        right = jnp.where(lane8 < H, edge, right)
        surface_halo[1, f] = jnp.where(far_depth[1] > 0.0, left, 0.0)
        surface_halo[2, f] = jnp.where(far_depth[2] > 0.0, right, 0.0)
    surface[0, 0] = jnp.where(depth[0] > 0.0, pack_middle(packed, lane), 0.0)
    surface_halo[0, 0] = jnp.where(far_depth[0] > 0.0, pack_middle(packed8, lane8), 0.0)

    for level in range(nl):
        p = (nt + 1) * nl + level
        for place in level_places(level, nl):
            at = pl.ds(place * 8, 8)
            far_weights[0, at, :] = halo_weights[0, at, :]
            far_weights[1, at, :], far_weights[2, at, :] = patched(
                p, halo_weights[1, at, :], halo_weights[2, at, :]
            )
        at = pl.ds(level * 8, 8)
        mid = halo_responses[0, at, :]
        near, far = patched(nt * nl + level, halo_responses[1, at, :], halo_responses[2, at, :])
        for place in level_places(level, nl):
            at = pl.ds((place - level // 8 * 8) * 8, 8)
            start_halo[level // 8, at, :] = (
                halo_jobs[level // 8, at, :] + mid * surface_halo[0, 0]
            )
        for f in range(nt):
            group, place = job_place(f, level, nl)
            at = pl.ds(place * 8, 8)
            left, right = patched(
                f * nl + level, halo_jobs[3 + group, at, :], halo_jobs[13 + group, at, :]
            )
            start_halo[3 + group, at, :] = left + near * surface_halo[1, f]
            start_halo[13 + group, at, :] = right + far * surface_halo[2, f]

    sub = lax.broadcasted_iota(jnp.int32, (8, 128), 0)

    def laplace(v, y):
        c = v[y]
        return (
            (v[y - 1] + v[y + 1]) + (pltpu.roll(c, 1, 1) + pltpu.roll(c, 127, 1))
        ) - 4.0 * c

    def begin(slot, job, part, first, f0, f4, values, at_job):
        for i in range(8):
            at = pl.ds(i * rows, rows)
            beside = pl.ds(pl.multiple_of((first + i) * rows, 8), rows)
            start[slot, pl.ds(i * PITCH, rows), :] = values[at_job, at, :] + responses[part, beside, :] * surface[
                part, f0 if i < 4 else f4
            ]
        level = (jnp.where(first == 16, sub & 3, sub) + first).astype(F32)
        v, w, stages = {}, {}, [{} for _ in range(2 * SUBSTEPS)]

        def update(now, y, change):
            if 0 <= y < rows:
                deep = depth[part, pl.ds(y, 1), :]
            else:
                deep = far_depth[part, pl.ds(y + 2 * H if y < 0 else y - rows, 1), :]
            return now[y] - jnp.where(level < deep, change, 0.0)

        def load(y):
            if 0 <= y < rows:
                v[y] = start[slot, pl.ds(y, 8, stride=PITCH), :]
                w[y] = weights[part, pl.ds(first * rows + y, 8, stride=rows), :]
            else:
                r = y + 2 * H if y < 0 else y - rows
                v[y] = start_halo[job, pl.ds(r, 8, stride=8), :]
                w[y] = far_weights[part, pl.ds(first * 8 + r, 8, stride=8), :]

        def advance(stage, y):
            k, edge = y, H - stage - 1
            if -edge <= k < rows + edge:
                now = v if stage < 2 else stages[stage // 2 * 2 - 1]
                if stage % 2 == 0:
                    stages[stage][k] = w[k] * laplace(now, k)
                else:
                    stages[stage][k] = update(now, k, laplace(stages[stage - 1], k))

        def store(k):
            if 0 <= k < rows:
                done[job, pl.ds(k, 8, stride=PITCH), :] = stages[-1][k]

        return load, advance, store

    def run(jobs):
        ys = range(-H, rows + H)
        for load, advance, store in jobs:
            for y in ys:
                load(y)
            for stage in range(2 * SUBSTEPS):
                for y in ys:
                    advance(stage, y)
            for y in ys:
                store(y)

    def strip(slot, m):
        return begin(slot, m, 0, 8 * m, 0, 0, mids, m)

    for m in range(3):
        run([strip(m % 2, jnp.int32(m))])

    def both(group, first, f0, f4):
        for half in range(2):
            job = 10 * half + group
            run([begin(half, 3 + job, 1 + half, first, f0, f4, sides, job)])
        for i in range(8):
            f = f0 if i < 4 else f4
            at = pl.ds(i * PITCH, rows)
            turn = pltpu.roll(done[first // 8, at, :], lax.rem(244 - 32 * f, 128), 1)
            merged[group, i, :, 0:128] = jnp.where(lane < 120, done[3 + group, at, :], turn)
            merged[group, i, :, 128:256] = jnp.where(lane >= 8, done[13 + group, at, :], turn)

    def whole_copy(group):
        first = pl.multiple_of(8 * (group % 2), 8)
        return pltpu.make_async_copy(
            merged.at[group], out.at[group // 2, pl.ds(first, 8)], sem.at[group, 0]
        )

    def half_copies(group):
        return [
            pltpu.make_async_copy(
                merged.at[group, pl.ds((nl - 16) * k, nl - 16)],
                out.at[2 * (group - 8) + k, pl.ds(16, nl - 16)],
                sem.at[group, k],
            )
            for k in range(2)
        ]

    def wholes(group):
        f = group // 2
        both(group, 8 * (group % 2), f, f)
        whole_copy(group).start()

    def pairs(group):
        f = 2 * (group - 8)
        both(group, 16 + 0 * group, f, f + 1)
        for copy in half_copies(group):
            copy.start()

    for group in range(8):
        wholes(jnp.int32(group))
    for group in range(8, 10):
        pairs(jnp.int32(group))
    for group in range(8):
        whole_copy(group).wait()
    for group in range(8, 10):
        for copy in half_copies(group):
            copy.wait()


def diffuse(arranged, main, side, north, south, nl):
    nt, rows, width = main.shape
    operands = (*arranged, main, side, north, south)
    return pl.pallas_call(
        functools.partial(diffuse_kernel, nl),
        out_shape=shaped(nt, nl, rows, width),
        in_specs=[VMEM] * len(operands),
        out_specs=ANY,
        scratch_shapes=[
            pltpu.VMEM((3, nt, rows, 128), F32),
            pltpu.VMEM((3, nt, 8, 128), F32),
            pltpu.VMEM((2, 8 * PITCH, 128), F32),
            pltpu.VMEM((23, 64, 128), F32),
            pltpu.VMEM((3, 24 * 8, 128), F32),
            pltpu.VMEM((3, 8, 128), F32),
            pltpu.VMEM((north.shape[0] - 3 * nt, 8, 128), F32),
            pltpu.VMEM((23, 8 * PITCH, 128), F32),
            pltpu.VMEM((10, 8, rows, width), F32),
            pltpu.SemaphoreType.DMA((10, 2)),
        ],
        compiler_params=params(DIFFUSE_MIB),
        name="diffuse",
    )(*operands)


def body(
    atm_flux,
    remap_weights,
    link_source,
    link_owner,
    link_block,
    ocean_mask,
    level_count,
    tracers,
    diffusivity,
    viscosity,
):
    n_oy = lax.axis_size("oy")
    n_ox = lax.axis_size("ox")
    devices = n_oy * n_ox
    nt, nl, rows, width = tracers.shape
    payload = remap(
        atm_flux, remap_weights, link_source, link_owner, link_block, devices, n_ox
    )
    arrived = lax.all_to_all(payload, ("oy", "ox"), split_axis=0, concat_axis=0, tiled=True)
    arrived = arrived.reshape(devices * (CAP + 1) * nt, 128)

    eastward = [(i, (i + 1) % n_ox) for i in range(n_ox)]
    westward = [(j, i) for i, j in eastward]
    southward = [(i, i + 1) for i in range(n_oy - 1)]
    northward = [(j, i) for i, j in southward]
    mids, sides, responses, weights, depth, west, east, top, bottom = mix(
        tracers, diffusivity, viscosity, ocean_mask, level_count
    )
    from_west = lax.ppermute(east, "ox", eastward)
    from_east = lax.ppermute(west, "ox", westward)
    north = lax.ppermute(bottom, "oy", southward)
    south = lax.ppermute(top, "oy", northward)
    arranged = arrange(
        nt, nl, (mids, sides, responses, weights, depth), (from_west, from_east, north, south)
    )
    strips = jnp.concatenate([from_west, from_east], axis=0)
    corners = jnp.concatenate([strips[:, :H], strips[:, rows - H :]], axis=1)
    ocean_flux, side, to_north, to_south = collect(arrived, ocean_mask, corners, nt)
    flux_north = lax.ppermute(to_south, "oy", southward)
    flux_south = lax.ppermute(to_north, "oy", northward)
    mixed = diffuse(arranged, ocean_flux, side, flux_north, flux_south, nl)
    return mixed, ocean_flux


def solution(mesh):
    placed = (
        P(("oy", "ox"), None, None),
        P(("oy", "ox"), None, None),
        P(("oy", "ox")),
        P(("oy", "ox"), None),
        P(("oy", "ox")),
        P("oy", "ox"),
        P("oy", "ox"),
        P(None, None, "oy", "ox"),
        P(None, "oy", "ox"),
        P(None, "oy", "ox"),
    )
    return jax.shard_map(
        body,
        mesh=mesh,
        in_specs=placed,
        out_specs=(P(None, None, "oy", "ox"), P(None, "oy", "ox")),
        check_vma=False,
    )
```

```python
import functools

import jax
import jax.numpy as jnp
from jax import lax
from jax.experimental import pallas as pl
from jax.experimental.pallas import tpu as pltpu
from jax.sharding import PartitionSpec as P

SUBSTEPS = 2
CAP = 6
H = 4
CHUNKS = 12
OWN_ID = 64
NBR_ID = 72
MIB = 1024 * 1024
PITCH = 40
MIX_MIB, ARRANGE_MIB, DIFFUSE_MIB = 60, 16, 24

VMEM = pl.BlockSpec(memory_space=pltpu.VMEM)
SMEM = pl.BlockSpec(memory_space=pltpu.SMEM)
ANY = pl.BlockSpec(memory_space=pl.ANY)
HBM = pl.BlockSpec(memory_space=pltpu.HBM)
F32 = jnp.float32
BF16 = jnp.bfloat16


def params(mib):
    return pltpu.CompilerParams(vmem_limit_bytes=mib * MIB)


def shaped(*shape):
    return jax.ShapeDtypeStruct(shape, F32)


def remap_kernel(
    n_ox, source, owner_row, block_row, flux, weights,
    payload, held, flux32, table, strips, codes, places, sem, sent,
):
    links = weights.shape[0]
    per = links // CHUNKS
    copies = [
        pltpu.make_async_copy(
            weights.at[pl.ds(c * per, per)], held.at[pl.ds(c * per, per)], sem.at[c]
        )
        for c in range(CHUNKS)
    ]
    for copy in copies:
        copy.start()
    devices = payload.shape[0]

    owners = owner_row[...]
    blocks = block_row[...].reshape(1, links)
    tiles = lax.broadcasted_iota(jnp.int32, (devices, links), 0)
    mine = tiles == owners
    onehot = mine.astype(BF16)
    before = (
        lax.broadcasted_iota(jnp.int32, (links, links), 0)
        < lax.broadcasted_iota(jnp.int32, (links, links), 1)
    ).astype(BF16)
    ranks = jnp.dot(onehot, before, preferred_element_type=F32)
    rank = jnp.sum(jnp.where(mine, ranks, 0.0), axis=0, keepdims=True).astype(jnp.int32)
    odds = blocks & 1
    columns = lax.rem(owners, n_ox)
    nbrs = owners - columns + lax.rem(columns + jnp.where(odds == 1, 1, n_ox - 1), n_ox)
    entries = rank + jnp.where(odds == 1, 0, CAP)
    codes[0:1, :] = owners
    codes[1:2, :] = rank
    codes[2:3, :] = nbrs
    codes[3:4, :] = entries
    codes[4:5, :] = (4 * entries + 4 * odds) & 127
    send = pltpu.make_async_copy(codes, places, sent)
    send.start()
    flux32[...] = flux[...].astype(F32)

    idents = (blocks + 1).astype(F32)
    spot = lax.broadcasted_iota(jnp.int32, (128, links), 0)
    across = (((1,), (1,)), ((), ()))
    table[...] = lax.dot_general(
        onehot,
        jnp.where(spot == OWN_ID + rank, idents, 0.0).astype(BF16),
        across,
        preferred_element_type=F32,
    ) + lax.dot_general(
        (tiles == nbrs).astype(BF16),
        jnp.where(spot == NBR_ID + entries, idents, 0.0).astype(BF16),
        across,
        preferred_element_type=F32,
    )

    def clear(i, carry):
        payload[i] = jnp.zeros(payload.shape[1:], F32)
        strips[i] = jnp.broadcast_to(table[pl.ds(i, 1), :], (4, 128))
        return carry

    lax.fori_loop(0, devices, clear, 0, unroll=4)
    send.wait()
    group = lax.broadcasted_iota(jnp.int32, (4, 128), 1) >> 2

    for c in range(CHUNKS):
        copies[c].wait()

        def chunk(_, carry, c=c):
            values, moves = [], []
            for k in range(c * per, (c + 1) * per, 2):
                two_x = jnp.concatenate([flux32[source[k]], flux32[source[k + 1]]], axis=0)
                two_w = jnp.concatenate([held[k], held[k + 1]], axis=1)
                product = jnp.dot(two_x.astype(BF16), two_w, preferred_element_type=F32)
                values += [(k, product[0:4, 0:128]), (k + 1, product[4:8, 128:256])]
            for k, value in values:
                payload[places[0, k], places[1, k]] = value
                moves.append((k, pltpu.roll(value, places[4, k], 1)))
            for k, moved in moves:
                nbr = places[2, k]
                strips[nbr] = jnp.where(group == places[3, k], moved, strips[nbr])
            return carry

        chunk(0, 0)

    def finish(i, carry):
        payload[i, CAP] = strips[i]
        return carry

    lax.fori_loop(0, devices, finish, 0, unroll=8)


def remap(flux, weights, source, owner, block, devices, n_ox):
    links = weights.shape[0]
    return pl.pallas_call(
        functools.partial(remap_kernel, n_ox),
        out_shape=shaped(devices, CAP + 1, 4, 128),
        in_specs=[SMEM, VMEM, VMEM, VMEM, ANY],
        out_specs=VMEM,
        scratch_shapes=[
            pltpu.VMEM((links, 128, 128), BF16),
            pltpu.VMEM(flux.shape, F32),
            pltpu.VMEM((devices, 128), F32),
            pltpu.VMEM((devices, 4, 128), F32),
            pltpu.VMEM((8, links), jnp.int32),
            pltpu.SMEM((8, links), jnp.int32),
            pltpu.SemaphoreType.DMA((CHUNKS,)),
            pltpu.SemaphoreType.DMA,
        ],
        compiler_params=params(60),
        name="remap",
    )(source, owner.T, block, flux, weights)


def job_place(f, level, nl):
    if level < 16:
        return 2 * f + level // 8, level % 8
    return 8 + f // 2, (f % 2) * (nl - 16) + level - 16


def level_places(level, nl):
    return (level,) if level < 16 else (level, level + nl - 16)


def middle(left, right, lane):
    return jnp.where(lane >= 64, left, right)


def spread_middle(mid, lane, nt):
    out = pltpu.roll(mid, 12, 1)
    for f in range(1, nt):
        out = jnp.where((lane >> 5) == f, pltpu.roll(mid, 32 * f + 12, 1), out)
    return out


def pack_middle(mids, lane):
    out = pltpu.roll(mids[0], 12, 1)
    for f in range(1, len(mids)):
        out = jnp.where((lane >> 5) == f, pltpu.roll(mids[f], 32 * f + 12, 1), out)
    return out


STORE = 400
MOVES = 23


def moves(store, mids, sides, responses, weights, depth, sem, back):
    rows = depth.shape[1]
    pairs = []
    for q, ref in enumerate((responses, weights)):
        for part in range(3):
            for third in range(3):
                block = ref.at[part, pl.ds(8 * rows * third, 8 * rows)]
                pairs.append((block, store.at[23 + 9 * q + 3 * part + third]))
    for part in range(3):
        pairs.append((depth.at[part], store.at[41 + part, pl.ds(0, rows)]))
    pairs.append((mids, store.at[pl.ds(0, 3)]))
    pairs.append((sides, store.at[pl.ds(3, 20)]))
    if back:
        pairs = [(b, a) for a, b in pairs]
    return [pltpu.make_async_copy(a, b, sem.at[k]) for k, (a, b) in enumerate(pairs)]


def mix_kernel(
    tracers, diffusivity, viscosity, mask, count,
    store, west, east, top, bottom,
    mids, sides, responses, weights, depth, ratios, sem,
):
    copies = moves(store, mids, sides, responses, weights, depth, sem, False)
    nt, nl, rows, width = tracers.shape
    levels = (count[...] * mask[...]).astype(F32)
    lane = lax.broadcasted_iota(jnp.int32, (rows, 128), 1)
    depth[1] = levels[:, 0:128]
    depth[2] = levels[:, 128:256]
    depth[0] = spread_middle(middle(levels[:, 0:128], levels[:, 128:256], lane), lane, nt)
    across = width // 128

    def tile(t, carry):
        first = pl.multiple_of((t // across) * 8, 8)
        half = t % across
        r = pl.ds(first, 8)
        c = pl.ds(pl.multiple_of(half * 128, 128), 128)

        def plane(f, level):
            group, place = job_place(f, level, nl)
            return 10 * half + group, pl.ds(first + place * rows, 8)

        bottomless = depth[1 + half, r, :]
        nothing = jnp.zeros((8, 128), F32)
        ratio, upper, single = nothing, nothing, nothing
        values = [nothing] * nt
        for level in range(nl):
            if level < nl - 1:
                lower = jnp.where(level + 1 < bottomless, diffusivity[level, r, c], 0.0)
            else:
                lower = nothing
            inverse = 1.0 / (1.0 + upper + lower + upper * ratio)
            ratio = -lower * inverse
            ratios[level] = ratio
            for f in range(nt):
                values[f] = (tracers[f, level, r, c] + upper * values[f]) * inverse
                at = plane(f, level)
                sides[at[0], at[1], :] = values[f]
            single = inverse if level == 0 else (upper * single) * inverse
            weight = jnp.where(level < bottomless, viscosity[level, r, c], 0.0)
            for place in level_places(level, nl):
                responses[1 + half, pl.ds(first + place * rows, 8), :] = single
                weights[1 + half, pl.ds(first + place * rows, 8), :] = weight
            upper = lower
        for level in range(nl - 2, -1, -1):
            ratio = ratios[level]
            for f in range(nt):
                at = plane(f, level)
                values[f] = sides[at[0], at[1], :] - ratio * values[f]
                sides[at[0], at[1], :] = values[f]
            single = responses[1 + half, pl.ds(first + level * rows, 8), :] - ratio * single
            for place in level_places(level, nl):
                responses[1 + half, pl.ds(first + place * rows, 8), :] = single
        return carry

    lax.fori_loop(0, rows // 8 * across, tile, 0)

    def halves(p):
        if p < nt * nl:
            group, place = job_place(p // nl, p % nl, nl)
            at = pl.ds(place * rows, rows)
            return sides[group, at, :], sides[10 + group, at, :]
        if p < (nt + 2) * nl:
            ref = (responses, weights)[p // nl - nt]
            at = pl.ds(p % nl * rows, rows)
            return ref[1, at, :], ref[2, at, :]
        return depth[1], depth[2]

    copies[MOVES - 1].start()
    part = lane >> 2
    planes = (nt + 2) * nl + 1
    for g in range(-(-planes // 32)):
        to_west = jnp.zeros((rows, 128), F32)
        to_east = jnp.zeros((rows, 128), F32)
        for s in range(min(32, planes - 32 * g)):
            p = 32 * g + s
            left, right = halves(p)
            to_west = jnp.where(part == s, pltpu.roll(left, 4 * s, 1), to_west)
            to_east = jnp.where(part == s, pltpu.roll(right, (4 * s + 4) % 128, 1), to_east)
            top[p, :, 0:128] = left[0:H]
            top[p, :, 128:256] = right[0:H]
            bottom[p, :, 0:128] = left[rows - H : rows]
            bottom[p, :, 128:256] = right[rows - H : rows]
        west[g] = to_west
        east[g] = to_east
    for level in range(nl):
        packed = pack_middle(
            [middle(*halves(f * nl + level), lane) for f in range(nt)], lane
        )
        for place in level_places(level, nl):
            mids[level // 8, pl.ds((place - level // 8 * 8) * rows, rows), :] = packed
        for q, ref in ((nt, responses), (nt + 1, weights)):
            spread = spread_middle(middle(*halves(q * nl + level), lane), lane, nt)
            for place in level_places(level, nl):
                ref[0, pl.ds(place * rows, rows), :] = spread
    for copy in copies[: MOVES - 1]:
        copy.start()
    for copy in copies:
        copy.wait()


def mix(tracers, diffusivity, viscosity, mask, count):
    nt, nl, rows, width = tracers.shape
    planes = (nt + 2) * nl + 1
    groups = -(-planes // 32)
    out = (
        shaped(STORE, 8 * rows, 128),
        shaped(groups, rows, 128),
        shaped(groups, rows, 128),
        shaped(planes, H, width),
        shaped(planes, H, width),
    )
    return pl.pallas_call(
        mix_kernel,
        out_shape=out,
        in_specs=[VMEM] * 5,
        out_specs=(HBM,) + (VMEM,) * 4,
        scratch_shapes=[
            pltpu.VMEM((3, 8 * rows, 128), F32),
            pltpu.VMEM((20, 8 * rows, 128), F32),
            pltpu.VMEM((3, 24 * rows, 128), F32),
            pltpu.VMEM((3, 24 * rows, 128), F32),
            pltpu.VMEM((3, rows, 128), F32),
            pltpu.VMEM((nl, 8, 128), F32),
            pltpu.SemaphoreType.DMA((MOVES,)),
        ],
        compiler_params=params(MIX_MIB),
        name="mix",
    )(tracers, diffusivity, viscosity, mask, count)


def arrange_kernel(
    nt, nl,
    store, west_in, east_in, north_in, south_in,
    mids, sides, responses, weights, depth,
    halo_jobs, halo_responses, halo_weights, halo_depth,
    from_west, from_east, north, south, sem, moved,
):
    pairs = (
        (west_in, from_west),
        (east_in, from_east),
        (north_in, north),
        (south_in, south),
    )
    copies = [pltpu.make_async_copy(a, b, sem.at[k]) for k, (a, b) in enumerate(pairs)]
    copies += moves(store, mids, sides, responses, weights, depth, moved, True)
    for copy in copies:
        copy.start()
    rows = depth.shape[1]
    lane = lax.broadcasted_iota(jnp.int32, (rows, 128), 1)
    lane8 = lax.broadcasted_iota(jnp.int32, (2 * H, 128), 1)

    def patch(p, ref, left, right, at):
        g, s = p // 32, p % 32
        ref[left, at, :] = jnp.where(
            lane >= 128 - H, pltpu.roll(from_west[g], (252 - 4 * s) % 128, 1), ref[left, at, :]
        )
        ref[right, at, :] = jnp.where(
            lane < H, pltpu.roll(from_east[g], (128 - 4 * s) % 128, 1), ref[right, at, :]
        )

    def beyond(p):
        both = jnp.concatenate([south[p], north[p]], axis=0)
        left, right = both[:, 0:128], both[:, 128:256]
        return left, right, middle(left, right, lane8)

    for copy in copies[:4]:
        copy.wait()
    for level in range(nl):
        packed = []
        for f in range(nt):
            group, place = job_place(f, level, nl)
            at = pl.ds(place * 8, 8)
            near, far, mid = beyond(f * nl + level)
            halo_jobs[3 + group, at, :] = near
            halo_jobs[13 + group, at, :] = far
            packed.append(mid)
        packed = pack_middle(packed, lane8)
        for place in level_places(level, nl):
            halo_jobs[level // 8, pl.ds((place - level // 8 * 8) * 8, 8), :] = packed
        for q, halo in ((nt, halo_responses), (nt + 1, halo_weights)):
            near, far, mid = beyond(q * nl + level)
            mid = spread_middle(mid, lane8, nt)
            for place in level_places(level, nl):
                at = pl.ds(place * 8, 8)
                halo[0, at, :] = mid
                halo[1, at, :] = near
                halo[2, at, :] = far
    near, far, mid = beyond((nt + 2) * nl)
    halo_depth[0] = spread_middle(mid, lane8, nt)
    halo_depth[1] = near
    halo_depth[2] = far
    for copy in copies[4:25]:
        copy.wait()
    for level in range(nl):
        for q, ref in ((nt, responses), (nt + 1, weights)):
            for place in level_places(level, nl):
                patch(q * nl + level, ref, 1, 2, pl.ds(place * rows, rows))
    patch((nt + 2) * nl, depth, 1, 2, slice(None))
    copies[26].wait()
    for level in range(nl):
        for f in range(nt):
            group, place = job_place(f, level, nl)
            patch(f * nl + level, sides, group, 10 + group, pl.ds(place * rows, rows))
    copies[25].wait()


def arrange(nt, nl, store, halo):
    operands = (store, *halo)
    rows = store.shape[1] // 8
    out = (
        shaped(3, 8 * rows, 128),
        shaped(20, 8 * rows, 128),
        shaped(3, 24 * rows, 128),
        shaped(3, 24 * rows, 128),
        shaped(3, rows, 128),
        shaped(23, 64, 128),
        shaped(3, 24 * 8, 128),
        shaped(3, 24 * 8, 128),
        shaped(3, 8, 128),
    )
    return pl.pallas_call(
        functools.partial(arrange_kernel, nt, nl),
        out_shape=out,
        in_specs=[HBM] * len(operands),
        out_specs=(VMEM,) * len(out),
        scratch_shapes=[pltpu.VMEM(x.shape, F32) for x in halo]
        + [pltpu.SemaphoreType.DMA((4,)), pltpu.SemaphoreType.DMA((MOVES,))],
        compiler_params=params(ARRANGE_MIB),
        name="arrange",
    )(*operands)


def two(x):
    high = x.astype(jnp.bfloat16)
    return high, (x - high.astype(jnp.float32)).astype(jnp.bfloat16)


def collect_kernel(
    arrived, mask, corners, ocean_flux, side, to_north, to_south,
):
    rows, width = mask.shape
    nt = ocean_flux.shape[0]
    stride = (CAP + 1) * nt
    devices = arrived.shape[0] // stride

    def slot(s):
        return jnp.concatenate(
            [arrived[pl.ds(s * nt + f, devices, stride=stride), :] for f in range(nt)], axis=1
        )

    idents = jnp.transpose(arrived[pl.ds(CAP * nt, devices, stride=stride), :]).astype(jnp.int32) - 1
    y = lax.broadcasted_iota(jnp.int32, (rows, devices), 0)
    places = jnp.concatenate([2 * y, 2 * y + 1], axis=0)
    total = jnp.zeros((2 * rows, nt * 128), jnp.float32)
    for s in range(CAP):
        pick = (places == idents[OWN_ID + s : OWN_ID + s + 1, :]).astype(jnp.bfloat16)
        for piece in two(slot(s)):
            total = total + jnp.dot(pick, piece, preferred_element_type=jnp.float32)
    keep = mask[...].astype(jnp.float32)
    main = []
    for f in range(nt):
        cells = slice(f * 128, (f + 1) * 128)
        main.append(jnp.concatenate([total[0:rows, cells], total[rows:, cells]], axis=1) * keep)
        ocean_flux[f] = main[f]
    pick = jnp.concatenate(
        [
            (y == (idents[NBR_ID + e : NBR_ID + e + 1, :] >> 1)).astype(jnp.bfloat16)
            for e in range(2 * CAP)
        ],
        axis=0,
    )
    high, low = two(slot(CAP))
    spread = jnp.dot(pick, high, preferred_element_type=jnp.float32) + jnp.dot(
        pick, low, preferred_element_type=jnp.float32
    )
    lane = lax.broadcasted_iota(jnp.int32, (rows, 128), 1)
    for f in range(nt):
        west = jnp.zeros((rows, 128), jnp.float32)
        east = jnp.zeros((rows, 128), jnp.float32)
        for e in range(CAP):
            part = spread[e * rows : (e + 1) * rows, f * 128 : (f + 1) * 128]
            west = west + pltpu.roll(part, (124 - 4 * e) % 128, 1)
            e = e + CAP
            part = spread[e * rows : (e + 1) * rows, f * 128 : (f + 1) * 128]
            east = east + pltpu.roll(part, (128 - 4 * e) % 128, 1)
        edge = jnp.where(lane < H, east, jnp.where(lane >= 128 - H, west, 0.0))
        side[f] = edge
        for t, lanes in enumerate((main[f][:, 0:128], main[f][:, 128:256], edge)):
            to_north[3 * f + t] = lanes[0:H]
            to_south[3 * f + t] = lanes[rows - H : rows]
    groups = corners.shape[0]
    for g in range(groups):
        to_north[3 * nt + g] = corners[g, 0:H]
        to_south[3 * nt + g] = corners[g, H : 2 * H]


def collect(arrived, mask, corners, nt):
    rows, width = mask.shape
    f32 = jnp.float32
    line = shaped(3 * nt + corners.shape[0], H, 128)
    return pl.pallas_call(
        collect_kernel,
        out_shape=(
            jax.ShapeDtypeStruct((nt, rows, width), f32),
            jax.ShapeDtypeStruct((nt, rows, 128), f32),
            line,
            line,
        ),
        in_specs=[VMEM] * 3,
        out_specs=(VMEM,) * 4,
        compiler_params=params(12),
        name="collect",
    )(arrived, mask, corners)


def diffuse_kernel(
    nl,
    mids, sides, responses, weights, depth,
    halo_jobs, halo_responses, halo_weights, halo_depth, main, side, north, south,
    out, surface, surface_halo, start, start_halo, far_weights, far_depth, corners,
    done, merged, sem,
):
    nt, rows, width = main.shape
    lane = lax.broadcasted_iota(jnp.int32, (rows, 128), 1)
    lane8 = lax.broadcasted_iota(jnp.int32, (2 * H, 128), 1)
    planes = (nt + 2) * nl + 1
    groups = -(-planes // 32)
    for g in range(2 * groups):
        corners[g] = jnp.concatenate([south[3 * nt + g], north[3 * nt + g]], axis=0)

    def patched(p, left, right):
        g, s = p // 32, p % 32
        return (
            jnp.where(lane8 >= 128 - H, pltpu.roll(corners[g], (252 - 4 * s) % 128, 1), left),
            jnp.where(lane8 < H, pltpu.roll(corners[groups + g], (128 - 4 * s) % 128, 1), right),
        )

    far_depth[0] = halo_depth[0]
    far_depth[1], far_depth[2] = patched(planes - 1, halo_depth[1], halo_depth[2])

    packed, packed8 = [], []
    for f in range(nt):
        left, right = main[f, :, 0:128], main[f, :, 128:256]
        packed.append(middle(left, right, lane))
        left = jnp.where(lane >= 128 - H, side[f], left)
        right = jnp.where(lane < H, side[f], right)
        surface[1, f] = jnp.where(depth[1] > 0.0, left, 0.0)
        surface[2, f] = jnp.where(depth[2] > 0.0, right, 0.0)
        left, right, edge = [
            jnp.concatenate([south[3 * f + t], north[3 * f + t]], axis=0) for t in range(3)
        ]
        packed8.append(middle(left, right, lane8))
        left = jnp.where(lane8 >= 128 - H, edge, left)
        right = jnp.where(lane8 < H, edge, right)
        surface_halo[1, f] = jnp.where(far_depth[1] > 0.0, left, 0.0)
        surface_halo[2, f] = jnp.where(far_depth[2] > 0.0, right, 0.0)
    surface[0, 0] = jnp.where(depth[0] > 0.0, pack_middle(packed, lane), 0.0)
    surface_halo[0, 0] = jnp.where(far_depth[0] > 0.0, pack_middle(packed8, lane8), 0.0)

    for level in range(nl):
        p = (nt + 1) * nl + level
        for place in level_places(level, nl):
            at = pl.ds(place * 8, 8)
            far_weights[0, at, :] = halo_weights[0, at, :]
            far_weights[1, at, :], far_weights[2, at, :] = patched(
                p, halo_weights[1, at, :], halo_weights[2, at, :]
            )
        at = pl.ds(level * 8, 8)
        mid = halo_responses[0, at, :]
        near, far = patched(nt * nl + level, halo_responses[1, at, :], halo_responses[2, at, :])
        for place in level_places(level, nl):
            at = pl.ds((place - level // 8 * 8) * 8, 8)
            start_halo[level // 8, at, :] = (
                halo_jobs[level // 8, at, :] + mid * surface_halo[0, 0]
            )
        for f in range(nt):
            group, place = job_place(f, level, nl)
            at = pl.ds(place * 8, 8)
            left, right = patched(
                f * nl + level, halo_jobs[3 + group, at, :], halo_jobs[13 + group, at, :]
            )
            start_halo[3 + group, at, :] = left + near * surface_halo[1, f]
            start_halo[13 + group, at, :] = right + far * surface_halo[2, f]

    sub = lax.broadcasted_iota(jnp.int32, (8, 128), 0)

    def laplace(v, y):
        c = v[y]
        return (
            (v[y - 1] + v[y + 1]) + (pltpu.roll(c, 1, 1) + pltpu.roll(c, 127, 1))
        ) - 4.0 * c

    def begin(slot, job, part, first, f0, f4, values, at_job):
        for i in range(8):
            at = pl.ds(i * rows, rows)
            beside = pl.ds(pl.multiple_of((first + i) * rows, 8), rows)
            start[slot, pl.ds(i * PITCH, rows), :] = values[at_job, at, :] + responses[part, beside, :] * surface[
                part, f0 if i < 4 else f4
            ]
        level = (jnp.where(first == 16, sub & 3, sub) + first).astype(F32)
        v, w, stages = {}, {}, [{} for _ in range(2 * SUBSTEPS)]

        def update(now, y, change):
            if 0 <= y < rows:
                deep = depth[part, pl.ds(y, 1), :]
            else:
                deep = far_depth[part, pl.ds(y + 2 * H if y < 0 else y - rows, 1), :]
            return now[y] - jnp.where(level < deep, change, 0.0)

        def load(y):
            if 0 <= y < rows:
                v[y] = start[slot, pl.ds(y, 8, stride=PITCH), :]
                w[y] = weights[part, pl.ds(first * rows + y, 8, stride=rows), :]
            else:
                r = y + 2 * H if y < 0 else y - rows
                v[y] = start_halo[job, pl.ds(r, 8, stride=8), :]
                w[y] = far_weights[part, pl.ds(first * 8 + r, 8, stride=8), :]

        def advance(stage, y):
            k, edge = y, H - stage - 1
            if -edge <= k < rows + edge:
                now = v if stage < 2 else stages[stage // 2 * 2 - 1]
                if stage % 2 == 0:
                    stages[stage][k] = w[k] * laplace(now, k)
                else:
                    stages[stage][k] = update(now, k, laplace(stages[stage - 1], k))

        def store(k):
            if 0 <= k < rows:
                done[job, pl.ds(k, 8, stride=PITCH), :] = stages[-1][k]

        return load, advance, store

    def run(jobs):
        ys = range(-H, rows + H)
        for load, advance, store in jobs:
            for y in ys:
                load(y)
            for stage in range(2 * SUBSTEPS):
                for y in ys:
                    advance(stage, y)
            for y in ys:
                store(y)

    def strip(slot, m):
        return begin(slot, m, 0, 8 * m, 0, 0, mids, m)

    for m in range(3):
        run([strip(m % 2, jnp.int32(m))])

    def both(group, first, f0, f4):
        for half in range(2):
            job = 10 * half + group
            run([begin(half, 3 + job, 1 + half, first, f0, f4, sides, job)])
        for i in range(8):
            f = f0 if i < 4 else f4
            at = pl.ds(i * PITCH, rows)
            turn = pltpu.roll(done[first // 8, at, :], lax.rem(244 - 32 * f, 128), 1)
            merged[group, i, :, 0:128] = jnp.where(lane < 120, done[3 + group, at, :], turn)
            merged[group, i, :, 128:256] = jnp.where(lane >= 8, done[13 + group, at, :], turn)

    def whole_copy(group):
        first = pl.multiple_of(8 * (group % 2), 8)
        return pltpu.make_async_copy(
            merged.at[group], out.at[group // 2, pl.ds(first, 8)], sem.at[group, 0]
        )

    def half_copies(group):
        return [
            pltpu.make_async_copy(
                merged.at[group, pl.ds((nl - 16) * k, nl - 16)],
                out.at[2 * (group - 8) + k, pl.ds(16, nl - 16)],
                sem.at[group, k],
            )
            for k in range(2)
        ]

    def wholes(group):
        f = group // 2
        both(group, 8 * (group % 2), f, f)
        whole_copy(group).start()

    def pairs(group):
        f = 2 * (group - 8)
        both(group, 16 + 0 * group, f, f + 1)
        for copy in half_copies(group):
            copy.start()

    for group in range(8):
        wholes(jnp.int32(group))
    for group in range(8, 10):
        pairs(jnp.int32(group))
    for group in range(8):
        whole_copy(group).wait()
    for group in range(8, 10):
        for copy in half_copies(group):
            copy.wait()


def diffuse(arranged, main, side, north, south, nl):
    nt, rows, width = main.shape
    operands = (*arranged, main, side, north, south)
    return pl.pallas_call(
        functools.partial(diffuse_kernel, nl),
        out_shape=shaped(nt, nl, rows, width),
        in_specs=[VMEM] * len(operands),
        out_specs=ANY,
        scratch_shapes=[
            pltpu.VMEM((3, nt, rows, 128), F32),
            pltpu.VMEM((3, nt, 8, 128), F32),
            pltpu.VMEM((2, 8 * PITCH, 128), F32),
            pltpu.VMEM((23, 64, 128), F32),
            pltpu.VMEM((3, 24 * 8, 128), F32),
            pltpu.VMEM((3, 8, 128), F32),
            pltpu.VMEM((north.shape[0] - 3 * nt, 8, 128), F32),
            pltpu.VMEM((23, 8 * PITCH, 128), F32),
            pltpu.VMEM((10, 8, rows, width), F32),
            pltpu.SemaphoreType.DMA((10, 2)),
        ],
        compiler_params=params(DIFFUSE_MIB),
        name="diffuse",
    )(*operands)


def body(
    atm_flux,
    remap_weights,
    link_source,
    link_owner,
    link_block,
    ocean_mask,
    level_count,
    tracers,
    diffusivity,
    viscosity,
):
    n_oy = lax.axis_size("oy")
    n_ox = lax.axis_size("ox")
    devices = n_oy * n_ox
    nt, nl, rows, width = tracers.shape
    payload = remap(
        atm_flux, remap_weights, link_source, link_owner, link_block, devices, n_ox
    )
    arrived = lax.all_to_all(payload, ("oy", "ox"), split_axis=0, concat_axis=0, tiled=True)
    arrived = arrived.reshape(devices * (CAP + 1) * nt, 128)

    eastward = [(i, (i + 1) % n_ox) for i in range(n_ox)]
    westward = [(j, i) for i, j in eastward]
    southward = [(i, i + 1) for i in range(n_oy - 1)]
    northward = [(j, i) for i, j in southward]
    store, west, east, top, bottom = mix(
        tracers, diffusivity, viscosity, ocean_mask, level_count
    )
    from_west = lax.ppermute(east, "ox", eastward)
    from_east = lax.ppermute(west, "ox", westward)
    north = lax.ppermute(bottom, "oy", southward)
    south = lax.ppermute(top, "oy", northward)
    arranged = arrange(nt, nl, store, (from_west, from_east, north, south))
    strips = jnp.concatenate([from_west, from_east], axis=0)
    corners = jnp.concatenate([strips[:, :H], strips[:, rows - H :]], axis=1)
    ocean_flux, side, to_north, to_south = collect(arrived, ocean_mask, corners, nt)
    flux_north = lax.ppermute(to_south, "oy", southward)
    flux_south = lax.ppermute(to_north, "oy", northward)
    mixed = diffuse(arranged, ocean_flux, side, flux_north, flux_south, nl)
    return mixed, ocean_flux


def solution(mesh):
    placed = (
        P(("oy", "ox"), None, None),
        P(("oy", "ox"), None, None),
        P(("oy", "ox")),
        P(("oy", "ox"), None),
        P(("oy", "ox")),
        P("oy", "ox"),
        P("oy", "ox"),
        P(None, None, "oy", "ox"),
        P(None, "oy", "ox"),
        P(None, "oy", "ox"),
    )
    return jax.shard_map(
        body,
        mesh=mesh,
        in_specs=placed,
        out_specs=(P(None, None, "oy", "ox"), P(None, "oy", "ox")),
        check_vma=False,
    )
```

```python
import functools

import jax
import jax.numpy as jnp
from jax import lax
from jax.experimental import pallas as pl
from jax.experimental.pallas import tpu as pltpu
from jax.sharding import PartitionSpec as P

SUBSTEPS = 2
CAP = 6
H = 4
CHUNKS = 12
OWN_ID = 64
NBR_ID = 72
MIB = 1024 * 1024
PITCH = 40
MIX_MIB, ARRANGE_MIB, DIFFUSE_MIB = 60, 16, 24

VMEM = pl.BlockSpec(memory_space=pltpu.VMEM)
SMEM = pl.BlockSpec(memory_space=pltpu.SMEM)
ANY = pl.BlockSpec(memory_space=pl.ANY)
HBM = pl.BlockSpec(memory_space=pltpu.HBM)
F32 = jnp.float32
BF16 = jnp.bfloat16


def params(mib):
    return pltpu.CompilerParams(vmem_limit_bytes=mib * MIB)


def shaped(*shape):
    return jax.ShapeDtypeStruct(shape, F32)


def remap_kernel(
    n_ox, source, owner_row, block_row, flux, weights,
    payload, held, flux32, table, strips, codes, places, sem, sent,
):
    links = weights.shape[0]
    per = links // CHUNKS
    copies = [
        pltpu.make_async_copy(
            weights.at[pl.ds(c * per, per)], held.at[pl.ds(c * per, per)], sem.at[c]
        )
        for c in range(CHUNKS)
    ]
    for copy in copies:
        copy.start()
    devices = payload.shape[0]

    owners = owner_row[...]
    blocks = block_row[...].reshape(1, links)
    tiles = lax.broadcasted_iota(jnp.int32, (devices, links), 0)
    mine = tiles == owners
    onehot = mine.astype(BF16)
    before = (
        lax.broadcasted_iota(jnp.int32, (links, links), 0)
        < lax.broadcasted_iota(jnp.int32, (links, links), 1)
    ).astype(BF16)
    ranks = jnp.dot(onehot, before, preferred_element_type=F32)
    rank = jnp.sum(jnp.where(mine, ranks, 0.0), axis=0, keepdims=True).astype(jnp.int32)
    odds = blocks & 1
    columns = lax.rem(owners, n_ox)
    nbrs = owners - columns + lax.rem(columns + jnp.where(odds == 1, 1, n_ox - 1), n_ox)
    entries = rank + jnp.where(odds == 1, 0, CAP)
    codes[0:1, :] = owners
    codes[1:2, :] = rank
    codes[2:3, :] = nbrs
    codes[3:4, :] = entries
    codes[4:5, :] = (4 * entries + 4 * odds) & 127
    send = pltpu.make_async_copy(codes, places, sent)
    send.start()
    flux32[...] = flux[...].astype(F32)

    idents = (blocks + 1).astype(F32)
    spot = lax.broadcasted_iota(jnp.int32, (128, links), 0)
    across = (((1,), (1,)), ((), ()))
    table[...] = lax.dot_general(
        onehot,
        jnp.where(spot == OWN_ID + rank, idents, 0.0).astype(BF16),
        across,
        preferred_element_type=F32,
    ) + lax.dot_general(
        (tiles == nbrs).astype(BF16),
        jnp.where(spot == NBR_ID + entries, idents, 0.0).astype(BF16),
        across,
        preferred_element_type=F32,
    )

    def clear(i, carry):
        payload[i] = jnp.zeros(payload.shape[1:], F32)
        strips[i] = jnp.broadcast_to(table[pl.ds(i, 1), :], (4, 128))
        return carry

    lax.fori_loop(0, devices, clear, 0, unroll=4)
    send.wait()
    group = lax.broadcasted_iota(jnp.int32, (4, 128), 1) >> 2

    for c in range(CHUNKS):
        copies[c].wait()

        def chunk(_, carry, c=c):
            values, moves = [], []
            for k in range(c * per, (c + 1) * per, 2):
                two_x = jnp.concatenate([flux32[source[k]], flux32[source[k + 1]]], axis=0)
                two_w = jnp.concatenate([held[k], held[k + 1]], axis=1)
                product = jnp.dot(two_x.astype(BF16), two_w, preferred_element_type=F32)
                values += [(k, product[0:4, 0:128]), (k + 1, product[4:8, 128:256])]
            for k, value in values:
                payload[places[0, k], places[1, k]] = value
                moves.append((k, pltpu.roll(value, places[4, k], 1)))
            for k, moved in moves:
                nbr = places[2, k]
                strips[nbr] = jnp.where(group == places[3, k], moved, strips[nbr])
            return carry

        chunk(0, 0)

    def finish(i, carry):
        payload[i, CAP] = strips[i]
        return carry

    lax.fori_loop(0, devices, finish, 0, unroll=8)


def remap(flux, weights, source, owner, block, devices, n_ox):
    links = weights.shape[0]
    return pl.pallas_call(
        functools.partial(remap_kernel, n_ox),
        out_shape=shaped(devices, CAP + 1, 4, 128),
        in_specs=[SMEM, VMEM, VMEM, VMEM, ANY],
        out_specs=VMEM,
        scratch_shapes=[
            pltpu.VMEM((links, 128, 128), BF16),
            pltpu.VMEM(flux.shape, F32),
            pltpu.VMEM((devices, 128), F32),
            pltpu.VMEM((devices, 4, 128), F32),
            pltpu.VMEM((8, links), jnp.int32),
            pltpu.SMEM((8, links), jnp.int32),
            pltpu.SemaphoreType.DMA((CHUNKS,)),
            pltpu.SemaphoreType.DMA,
        ],
        compiler_params=params(60),
        name="remap",
    )(source, owner.T, block, flux, weights)


def job_place(f, level, nl):
    if level < 16:
        return 2 * f + level // 8, level % 8
    return 8 + f // 2, (f % 2) * (nl - 16) + level - 16


def level_places(level, nl):
    return (level,) if level < 16 else (level, level + nl - 16)


def middle(left, right, lane):
    return jnp.where(lane >= 64, left, right)


def spread_middle(mid, lane, nt):
    out = pltpu.roll(mid, 12, 1)
    for f in range(1, nt):
        out = jnp.where((lane >> 5) == f, pltpu.roll(mid, 32 * f + 12, 1), out)
    return out


def pack_middle(mids, lane):
    out = pltpu.roll(mids[0], 12, 1)
    for f in range(1, len(mids)):
        out = jnp.where((lane >> 5) == f, pltpu.roll(mids[f], 32 * f + 12, 1), out)
    return out


STORE = 400
MOVES = 23


def moves(store, mids, sides, responses, weights, depth, sem, back):
    rows = depth.shape[1]
    pairs = []
    for q, ref in enumerate((responses, weights)):
        for part in range(3):
            for third in range(3):
                block = ref.at[part, pl.ds(8 * rows * third, 8 * rows)]
                pairs.append((block, store.at[23 + 9 * q + 3 * part + third]))
    for part in range(3):
        pairs.append((depth.at[part], store.at[41 + part, pl.ds(0, rows)]))
    pairs.append((mids, store.at[pl.ds(0, 3)]))
    pairs.append((sides, store.at[pl.ds(3, 20)]))
    if back:
        pairs = [(b, a) for a, b in pairs]
    return [pltpu.make_async_copy(a, b, sem.at[k]) for k, (a, b) in enumerate(pairs)]


def mix_kernel(
    tracers, diffusivity, viscosity, mask, count,
    store, west, east, top, bottom,
    mids, sides, responses, weights, depth, ratios, sem,
):
    copies = moves(store, mids, sides, responses, weights, depth, sem, False)
    nt, nl, rows, width = tracers.shape
    levels = (count[...] * mask[...]).astype(F32)
    lane = lax.broadcasted_iota(jnp.int32, (rows, 128), 1)
    depth[1] = levels[:, 0:128]
    depth[2] = levels[:, 128:256]
    depth[0] = spread_middle(middle(levels[:, 0:128], levels[:, 128:256], lane), lane, nt)
    across = width // 128

    def tile(t, carry):
        first = pl.multiple_of((t // across) * 8, 8)
        half = t % across
        r = pl.ds(first, 8)
        c = pl.ds(pl.multiple_of(half * 128, 128), 128)

        def plane(f, level):
            group, place = job_place(f, level, nl)
            return 10 * half + group, pl.ds(first + place * rows, 8)

        bottomless = depth[1 + half, r, :]
        nothing = jnp.zeros((8, 128), F32)
        ratio, upper, single = nothing, nothing, nothing
        values = [nothing] * nt
        for level in range(nl):
            if level < nl - 1:
                lower = jnp.where(level + 1 < bottomless, diffusivity[level, r, c], 0.0)
            else:
                lower = nothing
            inverse = 1.0 / (1.0 + upper + lower + upper * ratio)
            ratio = -lower * inverse
            ratios[level] = ratio
            for f in range(nt):
                values[f] = (tracers[f, level, r, c] + upper * values[f]) * inverse
                at = plane(f, level)
                sides[at[0], at[1], :] = values[f]
            single = inverse if level == 0 else (upper * single) * inverse
            weight = jnp.where(level < bottomless, viscosity[level, r, c], 0.0)
            for place in level_places(level, nl):
                responses[1 + half, pl.ds(first + place * rows, 8), :] = single
                weights[1 + half, pl.ds(first + place * rows, 8), :] = weight
            upper = lower
        for level in range(nl - 2, -1, -1):
            ratio = ratios[level]
            for f in range(nt):
                at = plane(f, level)
                values[f] = sides[at[0], at[1], :] - ratio * values[f]
                sides[at[0], at[1], :] = values[f]
            single = responses[1 + half, pl.ds(first + level * rows, 8), :] - ratio * single
            for place in level_places(level, nl):
                responses[1 + half, pl.ds(first + place * rows, 8), :] = single
        return carry

    lax.fori_loop(0, rows // 8 * across, tile, 0)

    def halves(p):
        if p < nt * nl:
            group, place = job_place(p // nl, p % nl, nl)
            at = pl.ds(place * rows, rows)
            return sides[group, at, :], sides[10 + group, at, :]
        if p < (nt + 2) * nl:
            ref = (responses, weights)[p // nl - nt]
            at = pl.ds(p % nl * rows, rows)
            return ref[1, at, :], ref[2, at, :]
        return depth[1], depth[2]

    copies[MOVES - 1].start()
    part = lane >> 2
    planes = (nt + 2) * nl + 1
    for g in range(-(-planes // 32)):
        to_west = jnp.zeros((rows, 128), F32)
        to_east = jnp.zeros((rows, 128), F32)
        for s in range(min(32, planes - 32 * g)):
            p = 32 * g + s
            left, right = halves(p)
            to_west = jnp.where(part == s, pltpu.roll(left, 4 * s, 1), to_west)
            to_east = jnp.where(part == s, pltpu.roll(right, (4 * s + 4) % 128, 1), to_east)
            top[p, :, 0:128] = left[0:H]
            top[p, :, 128:256] = right[0:H]
            bottom[p, :, 0:128] = left[rows - H : rows]
            bottom[p, :, 128:256] = right[rows - H : rows]
        west[g] = to_west
        east[g] = to_east
    for level in range(nl):
        packed = pack_middle(
            [middle(*halves(f * nl + level), lane) for f in range(nt)], lane
        )
        for place in level_places(level, nl):
            mids[level // 8, pl.ds((place - level // 8 * 8) * rows, rows), :] = packed
        for q, ref in ((nt, responses), (nt + 1, weights)):
            spread = spread_middle(middle(*halves(q * nl + level), lane), lane, nt)
            for place in level_places(level, nl):
                ref[0, pl.ds(place * rows, rows), :] = spread
    for copy in copies[: MOVES - 1]:
        copy.start()
    for copy in copies:
        copy.wait()


def mix(tracers, diffusivity, viscosity, mask, count):
    nt, nl, rows, width = tracers.shape
    planes = (nt + 2) * nl + 1
    groups = -(-planes // 32)
    out = (
        shaped(STORE, 8 * rows, 128),
        shaped(groups, rows, 128),
        shaped(groups, rows, 128),
        shaped(planes, H, width),
        shaped(planes, H, width),
    )
    return pl.pallas_call(
        mix_kernel,
        out_shape=out,
        in_specs=[VMEM] * 5,
        out_specs=(HBM,) + (VMEM,) * 4,
        scratch_shapes=[
            pltpu.VMEM((3, 8 * rows, 128), F32),
            pltpu.VMEM((20, 8 * rows, 128), F32),
            pltpu.VMEM((3, 24 * rows, 128), F32),
            pltpu.VMEM((3, 24 * rows, 128), F32),
            pltpu.VMEM((3, rows, 128), F32),
            pltpu.VMEM((nl, 8, 128), F32),
            pltpu.SemaphoreType.DMA((MOVES,)),
        ],
        compiler_params=params(MIX_MIB),
        name="mix",
    )(tracers, diffusivity, viscosity, mask, count)


def arrange_kernel(
    nt, nl,
    store, west_in, east_in, north_in, south_in,
    mids, sides, responses, weights, depth,
    halo_jobs, halo_responses, halo_weights, halo_depth,
    from_west, from_east, north, south, sem, moved,
):
    pairs = (
        (west_in, from_west),
        (east_in, from_east),
        (north_in, north),
        (south_in, south),
    )
    copies = [pltpu.make_async_copy(a, b, sem.at[k]) for k, (a, b) in enumerate(pairs)]
    copies += moves(store, mids, sides, responses, weights, depth, moved, True)
    copies = copies[:4] + copies[-1:] + copies[4:-1]
    for copy in copies:
        copy.start()
    rows = depth.shape[1]
    lane = lax.broadcasted_iota(jnp.int32, (rows, 128), 1)
    lane8 = lax.broadcasted_iota(jnp.int32, (2 * H, 128), 1)

    def patch(p, ref, left, right, at):
        g, s = p // 32, p % 32
        ref[left, at, :] = jnp.where(
            lane >= 128 - H, pltpu.roll(from_west[g], (252 - 4 * s) % 128, 1), ref[left, at, :]
        )
        ref[right, at, :] = jnp.where(
            lane < H, pltpu.roll(from_east[g], (128 - 4 * s) % 128, 1), ref[right, at, :]
        )

    def beyond(p):
        both = jnp.concatenate([south[p], north[p]], axis=0)
        left, right = both[:, 0:128], both[:, 128:256]
        return left, right, middle(left, right, lane8)

    for copy in copies[:4]:
        copy.wait()
    for level in range(nl):
        packed = []
        for f in range(nt):
            group, place = job_place(f, level, nl)
            at = pl.ds(place * 8, 8)
            near, far, mid = beyond(f * nl + level)
            halo_jobs[3 + group, at, :] = near
            halo_jobs[13 + group, at, :] = far
            packed.append(mid)
        packed = pack_middle(packed, lane8)
        for place in level_places(level, nl):
            halo_jobs[level // 8, pl.ds((place - level // 8 * 8) * 8, 8), :] = packed
        for q, halo in ((nt, halo_responses), (nt + 1, halo_weights)):
            near, far, mid = beyond(q * nl + level)
            mid = spread_middle(mid, lane8, nt)
            for place in level_places(level, nl):
                at = pl.ds(place * 8, 8)
                halo[0, at, :] = mid
                halo[1, at, :] = near
                halo[2, at, :] = far
    near, far, mid = beyond((nt + 2) * nl)
    halo_depth[0] = spread_middle(mid, lane8, nt)
    halo_depth[1] = near
    halo_depth[2] = far
    copies[4].wait()
    for level in range(nl):
        for f in range(nt):
            group, place = job_place(f, level, nl)
            patch(f * nl + level, sides, group, 10 + group, pl.ds(place * rows, rows))
    for copy in copies[5:26]:
        copy.wait()
    for level in range(nl):
        for q, ref in ((nt, responses), (nt + 1, weights)):
            for place in level_places(level, nl):
                patch(q * nl + level, ref, 1, 2, pl.ds(place * rows, rows))
    patch((nt + 2) * nl, depth, 1, 2, slice(None))
    copies[26].wait()


def arrange(nt, nl, store, halo):
    operands = (store, *halo)
    rows = store.shape[1] // 8
    out = (
        shaped(3, 8 * rows, 128),
        shaped(20, 8 * rows, 128),
        shaped(3, 24 * rows, 128),
        shaped(3, 24 * rows, 128),
        shaped(3, rows, 128),
        shaped(23, 64, 128),
        shaped(3, 24 * 8, 128),
        shaped(3, 24 * 8, 128),
        shaped(3, 8, 128),
    )
    return pl.pallas_call(
        functools.partial(arrange_kernel, nt, nl),
        out_shape=out,
        in_specs=[HBM] * len(operands),
        out_specs=(VMEM,) * len(out),
        scratch_shapes=[pltpu.VMEM(x.shape, F32) for x in halo]
        + [pltpu.SemaphoreType.DMA((4,)), pltpu.SemaphoreType.DMA((MOVES,))],
        compiler_params=params(ARRANGE_MIB),
        name="arrange",
    )(*operands)


def two(x):
    high = x.astype(jnp.bfloat16)
    return high, (x - high.astype(jnp.float32)).astype(jnp.bfloat16)


def collect_kernel(
    arrived, mask, corners, ocean_flux, side, to_north, to_south,
):
    rows, width = mask.shape
    nt = ocean_flux.shape[0]
    stride = (CAP + 1) * nt
    devices = arrived.shape[0] // stride

    def slot(s):
        return jnp.concatenate(
            [arrived[pl.ds(s * nt + f, devices, stride=stride), :] for f in range(nt)], axis=1
        )

    idents = jnp.transpose(arrived[pl.ds(CAP * nt, devices, stride=stride), :]).astype(jnp.int32) - 1
    y = lax.broadcasted_iota(jnp.int32, (rows, devices), 0)
    places = jnp.concatenate([2 * y, 2 * y + 1], axis=0)
    total = jnp.zeros((2 * rows, nt * 128), jnp.float32)
    for s in range(CAP):
        pick = (places == idents[OWN_ID + s : OWN_ID + s + 1, :]).astype(jnp.bfloat16)
        for piece in two(slot(s)):
            total = total + jnp.dot(pick, piece, preferred_element_type=jnp.float32)
    keep = mask[...].astype(jnp.float32)
    main = []
    for f in range(nt):
        cells = slice(f * 128, (f + 1) * 128)
        main.append(jnp.concatenate([total[0:rows, cells], total[rows:, cells]], axis=1) * keep)
        ocean_flux[f] = main[f]
    pick = jnp.concatenate(
        [
            (y == (idents[NBR_ID + e : NBR_ID + e + 1, :] >> 1)).astype(jnp.bfloat16)
            for e in range(2 * CAP)
        ],
        axis=0,
    )
    high, low = two(slot(CAP))
    spread = jnp.dot(pick, high, preferred_element_type=jnp.float32) + jnp.dot(
        pick, low, preferred_element_type=jnp.float32
    )
    lane = lax.broadcasted_iota(jnp.int32, (rows, 128), 1)
    for f in range(nt):
        west = jnp.zeros((rows, 128), jnp.float32)
        east = jnp.zeros((rows, 128), jnp.float32)
        for e in range(CAP):
            part = spread[e * rows : (e + 1) * rows, f * 128 : (f + 1) * 128]
            west = west + pltpu.roll(part, (124 - 4 * e) % 128, 1)
            e = e + CAP
            part = spread[e * rows : (e + 1) * rows, f * 128 : (f + 1) * 128]
            east = east + pltpu.roll(part, (128 - 4 * e) % 128, 1)
        edge = jnp.where(lane < H, east, jnp.where(lane >= 128 - H, west, 0.0))
        side[f] = edge
        for t, lanes in enumerate((main[f][:, 0:128], main[f][:, 128:256], edge)):
            to_north[3 * f + t] = lanes[0:H]
            to_south[3 * f + t] = lanes[rows - H : rows]
    groups = corners.shape[0]
    for g in range(groups):
        to_north[3 * nt + g] = corners[g, 0:H]
        to_south[3 * nt + g] = corners[g, H : 2 * H]


def collect(arrived, mask, corners, nt):
    rows, width = mask.shape
    f32 = jnp.float32
    line = shaped(3 * nt + corners.shape[0], H, 128)
    return pl.pallas_call(
        collect_kernel,
        out_shape=(
            jax.ShapeDtypeStruct((nt, rows, width), f32),
            jax.ShapeDtypeStruct((nt, rows, 128), f32),
            line,
            line,
        ),
        in_specs=[VMEM] * 3,
        out_specs=(VMEM,) * 4,
        compiler_params=params(12),
        name="collect",
    )(arrived, mask, corners)


def diffuse_kernel(
    nl,
    mids, sides, responses, weights, depth,
    halo_jobs, halo_responses, halo_weights, halo_depth, main, side, north, south,
    out, surface, surface_halo, start, start_halo, far_weights, far_depth, corners,
    done, merged, sem,
):
    nt, rows, width = main.shape
    lane = lax.broadcasted_iota(jnp.int32, (rows, 128), 1)
    lane8 = lax.broadcasted_iota(jnp.int32, (2 * H, 128), 1)
    planes = (nt + 2) * nl + 1
    groups = -(-planes // 32)
    for g in range(2 * groups):
        corners[g] = jnp.concatenate([south[3 * nt + g], north[3 * nt + g]], axis=0)

    def patched(p, left, right):
        g, s = p // 32, p % 32
        return (
            jnp.where(lane8 >= 128 - H, pltpu.roll(corners[g], (252 - 4 * s) % 128, 1), left),
            jnp.where(lane8 < H, pltpu.roll(corners[groups + g], (128 - 4 * s) % 128, 1), right),
        )

    far_depth[0] = halo_depth[0]
    far_depth[1], far_depth[2] = patched(planes - 1, halo_depth[1], halo_depth[2])

    packed, packed8 = [], []
    for f in range(nt):
        left, right = main[f, :, 0:128], main[f, :, 128:256]
        packed.append(middle(left, right, lane))
        left = jnp.where(lane >= 128 - H, side[f], left)
        right = jnp.where(lane < H, side[f], right)
        surface[1, f] = jnp.where(depth[1] > 0.0, left, 0.0)
        surface[2, f] = jnp.where(depth[2] > 0.0, right, 0.0)
        left, right, edge = [
            jnp.concatenate([south[3 * f + t], north[3 * f + t]], axis=0) for t in range(3)
        ]
        packed8.append(middle(left, right, lane8))
        left = jnp.where(lane8 >= 128 - H, edge, left)
        right = jnp.where(lane8 < H, edge, right)
        surface_halo[1, f] = jnp.where(far_depth[1] > 0.0, left, 0.0)
        surface_halo[2, f] = jnp.where(far_depth[2] > 0.0, right, 0.0)
    surface[0, 0] = jnp.where(depth[0] > 0.0, pack_middle(packed, lane), 0.0)
    surface_halo[0, 0] = jnp.where(far_depth[0] > 0.0, pack_middle(packed8, lane8), 0.0)

    for level in range(nl):
        p = (nt + 1) * nl + level
        for place in level_places(level, nl):
            at = pl.ds(place * 8, 8)
            far_weights[0, at, :] = halo_weights[0, at, :]
            far_weights[1, at, :], far_weights[2, at, :] = patched(
                p, halo_weights[1, at, :], halo_weights[2, at, :]
            )
        at = pl.ds(level * 8, 8)
        mid = halo_responses[0, at, :]
        near, far = patched(nt * nl + level, halo_responses[1, at, :], halo_responses[2, at, :])
        for place in level_places(level, nl):
            at = pl.ds((place - level // 8 * 8) * 8, 8)
            start_halo[level // 8, at, :] = (
                halo_jobs[level // 8, at, :] + mid * surface_halo[0, 0]
            )
        for f in range(nt):
            group, place = job_place(f, level, nl)
            at = pl.ds(place * 8, 8)
            left, right = patched(
                f * nl + level, halo_jobs[3 + group, at, :], halo_jobs[13 + group, at, :]
            )
            start_halo[3 + group, at, :] = left + near * surface_halo[1, f]
            start_halo[13 + group, at, :] = right + far * surface_halo[2, f]

    sub = lax.broadcasted_iota(jnp.int32, (8, 128), 0)

    def laplace(v, y):
        c = v[y]
        return (
            (v[y - 1] + v[y + 1]) + (pltpu.roll(c, 1, 1) + pltpu.roll(c, 127, 1))
        ) - 4.0 * c

    def begin(slot, job, part, first, f0, f4, values, at_job):
        for i in range(8):
            at = pl.ds(i * rows, rows)
            beside = pl.ds(pl.multiple_of((first + i) * rows, 8), rows)
            start[slot, pl.ds(i * PITCH, rows), :] = values[at_job, at, :] + responses[part, beside, :] * surface[
                part, f0 if i < 4 else f4
            ]
        level = (jnp.where(first == 16, sub & 3, sub) + first).astype(F32)
        v, w, stages = {}, {}, [{} for _ in range(2 * SUBSTEPS)]

        def update(now, y, change):
            if 0 <= y < rows:
                deep = depth[part, pl.ds(y, 1), :]
            else:
                deep = far_depth[part, pl.ds(y + 2 * H if y < 0 else y - rows, 1), :]
            return now[y] - jnp.where(level < deep, change, 0.0)

        def load(y):
            if 0 <= y < rows:
                v[y] = start[slot, pl.ds(y, 8, stride=PITCH), :]
                w[y] = weights[part, pl.ds(first * rows + y, 8, stride=rows), :]
            else:
                r = y + 2 * H if y < 0 else y - rows
                v[y] = start_halo[job, pl.ds(r, 8, stride=8), :]
                w[y] = far_weights[part, pl.ds(first * 8 + r, 8, stride=8), :]

        def advance(stage, y):
            k, edge = y, H - stage - 1
            if -edge <= k < rows + edge:
                now = v if stage < 2 else stages[stage // 2 * 2 - 1]
                if stage % 2 == 0:
                    stages[stage][k] = w[k] * laplace(now, k)
                else:
                    stages[stage][k] = update(now, k, laplace(stages[stage - 1], k))

        def store(k):
            if 0 <= k < rows:
                done[job, pl.ds(k, 8, stride=PITCH), :] = stages[-1][k]

        return load, advance, store

    def run(jobs):
        ys = range(-H, rows + H)
        for load, advance, store in jobs:
            for y in ys:
                load(y)
            for stage in range(2 * SUBSTEPS):
                for y in ys:
                    advance(stage, y)
            for y in ys:
                store(y)

    def strip(slot, m):
        return begin(slot, m, 0, 8 * m, 0, 0, mids, m)

    for m in range(3):
        run([strip(m % 2, jnp.int32(m))])

    def both(group, first, f0, f4):
        for half in range(2):
            job = 10 * half + group
            run([begin(half, 3 + job, 1 + half, first, f0, f4, sides, job)])
        for i in range(8):
            f = f0 if i < 4 else f4
            at = pl.ds(i * PITCH, rows)
            turn = pltpu.roll(done[first // 8, at, :], lax.rem(244 - 32 * f, 128), 1)
            merged[group, i, :, 0:128] = jnp.where(lane < 120, done[3 + group, at, :], turn)
            merged[group, i, :, 128:256] = jnp.where(lane >= 8, done[13 + group, at, :], turn)

    def whole_copy(group):
        first = pl.multiple_of(8 * (group % 2), 8)
        return pltpu.make_async_copy(
            merged.at[group], out.at[group // 2, pl.ds(first, 8)], sem.at[group, 0]
        )

    def half_copies(group):
        return [
            pltpu.make_async_copy(
                merged.at[group, pl.ds((nl - 16) * k, nl - 16)],
                out.at[2 * (group - 8) + k, pl.ds(16, nl - 16)],
                sem.at[group, k],
            )
            for k in range(2)
        ]

    def wholes(group):
        f = group // 2
        both(group, 8 * (group % 2), f, f)
        whole_copy(group).start()

    def pairs(group):
        f = 2 * (group - 8)
        both(group, 16 + 0 * group, f, f + 1)
        for copy in half_copies(group):
            copy.start()

    for group in range(8):
        wholes(jnp.int32(group))
    for group in range(8, 10):
        pairs(jnp.int32(group))
    for group in range(8):
        whole_copy(group).wait()
    for group in range(8, 10):
        for copy in half_copies(group):
            copy.wait()


def diffuse(arranged, main, side, north, south, nl):
    nt, rows, width = main.shape
    operands = (*arranged, main, side, north, south)
    return pl.pallas_call(
        functools.partial(diffuse_kernel, nl),
        out_shape=shaped(nt, nl, rows, width),
        in_specs=[VMEM] * len(operands),
        out_specs=ANY,
        scratch_shapes=[
            pltpu.VMEM((3, nt, rows, 128), F32),
            pltpu.VMEM((3, nt, 8, 128), F32),
            pltpu.VMEM((2, 8 * PITCH, 128), F32),
            pltpu.VMEM((23, 64, 128), F32),
            pltpu.VMEM((3, 24 * 8, 128), F32),
            pltpu.VMEM((3, 8, 128), F32),
            pltpu.VMEM((north.shape[0] - 3 * nt, 8, 128), F32),
            pltpu.VMEM((23, 8 * PITCH, 128), F32),
            pltpu.VMEM((10, 8, rows, width), F32),
            pltpu.SemaphoreType.DMA((10, 2)),
        ],
        compiler_params=params(DIFFUSE_MIB),
        name="diffuse",
    )(*operands)


def body(
    atm_flux,
    remap_weights,
    link_source,
    link_owner,
    link_block,
    ocean_mask,
    level_count,
    tracers,
    diffusivity,
    viscosity,
):
    n_oy = lax.axis_size("oy")
    n_ox = lax.axis_size("ox")
    devices = n_oy * n_ox
    nt, nl, rows, width = tracers.shape
    payload = remap(
        atm_flux, remap_weights, link_source, link_owner, link_block, devices, n_ox
    )
    arrived = lax.all_to_all(payload, ("oy", "ox"), split_axis=0, concat_axis=0, tiled=True)
    arrived = arrived.reshape(devices * (CAP + 1) * nt, 128)

    eastward = [(i, (i + 1) % n_ox) for i in range(n_ox)]
    westward = [(j, i) for i, j in eastward]
    southward = [(i, i + 1) for i in range(n_oy - 1)]
    northward = [(j, i) for i, j in southward]
    store, west, east, top, bottom = mix(
        tracers, diffusivity, viscosity, ocean_mask, level_count
    )
    from_west = lax.ppermute(east, "ox", eastward)
    from_east = lax.ppermute(west, "ox", westward)
    north = lax.ppermute(bottom, "oy", southward)
    south = lax.ppermute(top, "oy", northward)
    arranged = arrange(nt, nl, store, (from_west, from_east, north, south))
    strips = jnp.concatenate([from_west, from_east], axis=0)
    corners = jnp.concatenate([strips[:, :H], strips[:, rows - H :]], axis=1)
    ocean_flux, side, to_north, to_south = collect(arrived, ocean_mask, corners, nt)
    flux_north = lax.ppermute(to_south, "oy", southward)
    flux_south = lax.ppermute(to_north, "oy", northward)
    mixed = diffuse(arranged, ocean_flux, side, flux_north, flux_south, nl)
    return mixed, ocean_flux


def solution(mesh):
    placed = (
        P(("oy", "ox"), None, None),
        P(("oy", "ox"), None, None),
        P(("oy", "ox")),
        P(("oy", "ox"), None),
        P(("oy", "ox")),
        P("oy", "ox"),
        P("oy", "ox"),
        P(None, None, "oy", "ox"),
        P(None, "oy", "ox"),
        P(None, "oy", "ox"),
    )
    return jax.shard_map(
        body,
        mesh=mesh,
        in_specs=placed,
        out_specs=(P(None, None, "oy", "ox"), P(None, "oy", "ox")),
        check_vma=False,
    )
```
